256 devices in a mesh: tx: 8 (over z), ty: 32 (over x, y, core).
Axes of the slice: x: 4, y: 4, z: 8, core: 2. Of those that a mesh axis runs over, the one named last changes fastest.
Arguments:
- source: bfloat16 [512, 2048, 2, 128], P('tx', 'ty'), may hold values from -6 to 6
- guess: bfloat16 [512, 2048, 2, 128], P('tx', 'ty'), may hold values from -6 to 6
- coefficient: float32 [512, 2048], P('tx', 'ty'), may hold values from 0.25 to 2.5
- leaf_map: float32 [8, 32, 2, 256, 256], P('tx', 'ty'), may hold values from -0.9 to 0.9, as said below
- body_map: bfloat16 [8, 32, 2, 256, 4096], P('tx', 'ty'), may hold values from -0.013671875 to 0.013671875
Outputs:
- top_map: float32 [8, 32, 2, 64, 768], P('tx', 'ty')
- top_outgoing: float32 [8, 32, 2, 64, 128], P('tx', 'ty')
The draws below stay inside these ranges and needn't reach their ends.
Inputs may be any that keep to these rules, and one draw needn't show every extreme that they name: `leaf_map`: as a complex matrix, each tile's map has spectral norm at most 0.9.
All inputs are finite; a program needn't handle non-finite values.
Results may differ from the reference program's by a relative error of at most 0.0029.
Values may be sent and summed in bfloat16 or wider, within the bound.
No kernel may reach another device: no remote copies, remote signals or barrier semaphores. Data moves between devices by JAX's collectives and lax.ppermute only.
A program may use at most 64 MiB of HBM per device.

```python
import math
from functools import partial
import jax
import jax.numpy as jnp
import numpy as np
from jax import lax

TILE = 64
RHS = 128
TILE_ROWS = 8
TILE_COLS = 32
NX = 512
NY = 2048
ORDER = 256
CELLS = 4096


def cayley_embedded(real_draw, imag_draw):
    skew_real = (real_draw - real_draw.T) / math.sqrt(2.0)
    sym_imag = (imag_draw + imag_draw.T) / math.sqrt(2.0)
    upper_half = jnp.concatenate([skew_real, -sym_imag], axis=1)
    lower_half = jnp.concatenate([sym_imag, skew_real], axis=1)
    embedded = jnp.concatenate([upper_half, lower_half], axis=0)
    identity = jnp.eye(embedded.shape[0], dtype=jnp.float32)
    return jnp.linalg.solve(identity + embedded, identity - embedded)


def leaf_tile(tile_key):
    sub_keys = jax.random.split(tile_key, 2)
    random_parts = jax.random.normal(sub_keys[0], (4, ORDER, ORDER), jnp.float32)
    lowest = 0.8
    side_index = jnp.arange(ORDER) // TILE
    same_side = (side_index[:, None] == side_index[None, :]).astype(jnp.float32)
    other_side = 1.0 - same_side
    side_scale = 2.0 / math.sqrt(TILE)
    mix_scale = 0.32 / math.sqrt(ORDER)
    side_unitary = cayley_embedded(random_parts[0] * same_side * side_scale, random_parts[1] * same_side * side_scale)
    mix_unitary = cayley_embedded(random_parts[2] * other_side * mix_scale, random_parts[3] * other_side * mix_scale)
    unitary = jnp.dot(side_unitary, mix_unitary, precision=lax.Precision.HIGHEST, preferred_element_type=jnp.float32)
    column_scales = jnp.exp(jax.random.uniform(sub_keys[1], (ORDER,), jnp.float32, math.log(lowest), math.log(0.9)))
    real_block = unitary[:ORDER, :ORDER] * column_scales[None, :]
    imag_block = unitary[ORDER:, :ORDER] * column_scales[None, :]
    return jnp.stack([real_block, imag_block])


def draw_leaf_map(key, part):
    tile_keys = jax.random.split(key, TILE_ROWS * TILE_COLS)
    tiles_all = lax.map(leaf_tile, tile_keys)
    return tiles_all.reshape(TILE_ROWS, TILE_COLS, 2, ORDER, ORDER)


def level_of(stream_key, shape, cuts, low, largest):
    loudness = 1.0
    for position, parts in cuts:
        steps = jax.random.uniform(jax.random.fold_in(jax.random.fold_in(stream_key, 6), position), (parts,), jnp.float32, low / len(cuts), largest / len(cuts))
        loudness = loudness * jnp.repeat(jnp.exp(steps), shape[position] // parts).reshape((-1,) + (1,) * (len(shape) - 1 - position))
    return loudness


def noise(rng, shape, scale, most, shards=(), kind=jnp.bfloat16):
    loudness = level_of(rng, shape, shards, -0.22, 0.18) if shards else 1.0
    entries = jax.random.normal(rng, shape, jnp.float32) * scale * loudness
    return jnp.minimum(jnp.maximum(entries, -most), most).astype(kind)


def setup_inputs(seed: int = 0) -> dict:
    key_of = jax.random.split(jax.random.key(seed), 6)
    source = noise(key_of[0], (NX, NY, 2, RHS), 1.0, 6.0, ((0, 8), (1, 32)))
    guess = noise(key_of[1], (NX, NY, 2, RHS), 1.0, 6.0, ((0, 8), (1, 32)))
    coefficient = jnp.clip(jnp.exp(math.log(2.5) - 2.3025851 * jax.random.uniform(key_of[2], (NX, NY), jnp.float32) ** level_of(key_of[2], (NX, NY), ((0, 8), (1, 32)), -0.2, 0.2)), 0.25, 2.5)
    leaf_map = draw_leaf_map(jax.random.fold_in(key_of[5], 71), 0)
    body_map = noise(key_of[4], (TILE_ROWS, TILE_COLS, 2, ORDER, CELLS), (50 * CELLS) ** -0.5, 0.013671875, ((0, 8), (1, 32)))
    return {"source": source, "guess": guess, "coefficient": coefficient, "leaf_map": leaf_map, "body_map": body_map}


DAMPING = 0.5
SQUARINGS = 8

def matmul_high(left, right):
    return jnp.dot(left.astype(jnp.float32), right.astype(jnp.float32), precision=lax.Precision.HIGHEST, preferred_element_type=jnp.float32)

def complex_dot(left, right):
    real_part = matmul_high(left[0], right[0]) - matmul_high(left[1], right[1])
    imag_part = matmul_high(left[0], right[1]) + matmul_high(left[1], right[0])
    return jnp.stack([real_part, imag_part])

def complex_solve(reflect, right_part):
    answer = right_part
    power = reflect
    for step_num in range(SQUARINGS):
        answer = answer + complex_dot(power, answer)
        if step_num + 1 < SQUARINGS:
            power = complex_dot(power, power)
    return answer

def side_pieces(side_counts, tile_len):
    pieces = []
    offset = 0
    for segments in side_counts:
        pieces.append((offset, segments * tile_len))
        offset = offset + segments * tile_len
    return pieces

def select_pieces(matrix, pieces, axis_num):
    return jnp.concatenate([lax.slice_in_dim(matrix, begin_at, begin_at + length, axis=axis_num) for begin_at, length in pieces], axis=axis_num)

def face_sides(vertical):
    if vertical:
        return (2, 0)
    return (1, 3)

def interface_coef(face_a, face_out_a, face_b, face_out_b, ext_a, ext_b, side_a, side_b):
    cross_a = select_pieces(face_a, ext_a, 2)
    inner_a = select_pieces(face_a, [side_a], 2)
    cross_b = select_pieces(face_b, ext_b, 2)
    inner_b = select_pieces(face_b, [side_b], 2)
    product = complex_dot(inner_b, inner_a)
    right_part = jnp.concatenate([complex_dot(inner_b, cross_a), -cross_b, complex_dot(inner_b, face_out_a) - face_out_b], axis=2)
    return complex_solve(product, right_part)

def interface_wave(face_a, face_out_a, coeffs, ext_a, side_a, len_b):
    cross_a = select_pieces(face_a, ext_a, 2)
    inner_a = select_pieces(face_a, [side_a], 2)
    filler = jnp.zeros((2, cross_a.shape[1], len_b), jnp.float32)
    return -jnp.concatenate([cross_a, filler, face_out_a], axis=2) - complex_dot(inner_a, coeffs)

def rows_first(rows_map, rows_out, coeffs, ext_a, side_a, len_b):
    local_part = select_pieces(rows_map, ext_a, 2)
    across = select_pieces(rows_map, [side_a], 2)
    filler = jnp.zeros((2, rows_map.shape[1], len_b), jnp.float32)
    return complex_dot(across, coeffs) + jnp.concatenate([local_part, filler, rows_out], axis=2)

def rows_second(rows_map, rows_out, waves, ext_b, side_b, len_a):
    local_part = select_pieces(rows_map, ext_b, 2)
    across = select_pieces(rows_map, [side_b], 2)
    filler = jnp.zeros((2, rows_map.shape[1], len_a), jnp.float32)
    return complex_dot(across, waves) + jnp.concatenate([filler, local_part, rows_out], axis=2)

def merge_pair(map_a, out_a, map_b, out_b, side_counts, vertical, tile_len):
    pieces = side_pieces(side_counts, tile_len)
    idx_a, idx_b = face_sides(vertical)
    ext_a = [pieces[k] for k in range(4) if k != idx_a]
    ext_b = [pieces[k] for k in range(4) if k != idx_b]
    len_a = sum((p[1] for p in ext_a))
    len_b = sum((p[1] for p in ext_b))
    face_a = select_pieces(map_a, [pieces[idx_a]], 1)
    face_out_a = select_pieces(out_a, [pieces[idx_a]], 1)
    face_b = select_pieces(map_b, [pieces[idx_b]], 1)
    face_out_b = select_pieces(out_b, [pieces[idx_b]], 1)
    coeffs = interface_coef(face_a, face_out_a, face_b, face_out_b, ext_a, ext_b, pieces[idx_a], pieces[idx_b])
    waves = interface_wave(face_a, face_out_a, coeffs, ext_a, pieces[idx_a], len_b)
    upper_rows = rows_first(select_pieces(map_a, ext_a, 1), select_pieces(out_a, ext_a, 1), coeffs, ext_a, pieces[idx_a], len_b)
    lower_rows = rows_second(select_pieces(map_b, ext_b, 1), select_pieces(out_b, ext_b, 1), waves, ext_b, pieces[idx_b], len_a)
    joined = jnp.concatenate([upper_rows, lower_rows], axis=1)
    map_cols = len_a + len_b
    return (joined[:, :, :map_cols], joined[:, :, map_cols:])

def canonical_order(side_counts, vertical, tile_len):
    south_len, east_len, north_len, west_len = [c * tile_len for c in side_counts]
    if vertical:
        lengths = [south_len, east_len, west_len, east_len, north_len, west_len]
        sequence = [0, 1, 3, 4, 2, 5]
        merged = (side_counts[0], 2 * side_counts[1], side_counts[2], 2 * side_counts[3])
    else:
        lengths = [south_len, north_len, west_len, south_len, east_len, north_len]
        sequence = [0, 3, 4, 1, 5, 2]
        merged = (2 * side_counts[0], side_counts[1], 2 * side_counts[2], side_counts[3])
    begins = [sum(lengths[:k]) for k in range(6)]
    return ([(begins[k], lengths[k]) for k in sequence], merged)

def reorder_box(box_map, box_out, pieces):
    return (select_pieces(select_pieces(box_map, pieces, 1), pieces, 2), select_pieces(box_out, pieces, 1))

def residual_of(source, padded, coefficient):
    center = padded[1:-1, 1:-1]
    beside_all = padded[2:, 1:-1] + padded[:-2, 1:-1] + padded[1:-1, 2:] + padded[1:-1, :-2]
    wave_term = coefficient[:, :, None]
    diagonal_term = 4.0 - wave_term
    real_part = diagonal_term * center[:, :, 0] + wave_term * DAMPING * center[:, :, 1] - beside_all[:, :, 0]
    imag_part = diagonal_term * center[:, :, 1] - wave_term * DAMPING * center[:, :, 0] - beside_all[:, :, 1]
    applied = jnp.stack([real_part, imag_part], axis=2)
    return (source.astype(jnp.float32) - applied).astype(jnp.bfloat16)

def leaf_rows(inputs):
    maps_row, cells_row = inputs
    products = jnp.einsum('tack,tkbr->tabcr', maps_row.astype(jnp.float32), cells_row.astype(jnp.float32), precision=lax.Precision.HIGHEST)
    real_part = products[:, 0, 0] - products[:, 1, 1]
    imag_part = products[:, 0, 1] + products[:, 1, 0]
    return jnp.stack([real_part, imag_part], axis=1)

def flatten_grid(matrix):
    return matrix.reshape((-1,) + matrix.shape[2:])

def spread_rows(top_arrays):
    seg_table = np.array([[0, 1], [5, 3], [10, 6], [8, 9]])
    blocks = top_arrays.reshape(top_arrays.shape[:3] + (12, TILE, top_arrays.shape[-1]))
    chosen = blocks[:, :, :, seg_table]
    return chosen.transpose(0, 3, 1, 4, 2, 5, 6).reshape(TILE_ROWS, TILE_COLS, 2, TILE, top_arrays.shape[-1])

def reference(source, guess, coefficient, leaf_map, body_map):
    padded = jnp.pad(guess.astype(jnp.float32), ((1, 1), (1, 1), (0, 0), (0, 0)))
    residual = residual_of(source, padded, coefficient)
    cells = residual.reshape(TILE_ROWS, TILE, TILE_COLS, TILE, 2, RHS).transpose(0, 2, 1, 3, 4, 5).reshape(TILE_ROWS, TILE_COLS, CELLS, 2, RHS)
    outgoing = lax.map(leaf_rows, (body_map, cells))
    maps = leaf_map
    side_counts = (1, 1, 1, 1)
    for layer_idx in range(3):
        vertical = layer_idx % 2 == 0
        if vertical:
            map_a, map_b = (maps[0::2], maps[1::2])
            out_a, out_b = (outgoing[0::2], outgoing[1::2])
        else:
            map_a, map_b = (maps[:, 0::2], maps[:, 1::2])
            out_a, out_b = (outgoing[:, 0::2], outgoing[:, 1::2])
        grid_shape = map_a.shape[:2]
        merge_fn = partial(merge_pair, side_counts=side_counts, vertical=vertical, tile_len=TILE)
        new_maps, new_out = jax.vmap(merge_fn)(flatten_grid(map_a), flatten_grid(out_a), flatten_grid(map_b), flatten_grid(out_b))
        if layer_idx < 2:
            pieces, side_counts = canonical_order(side_counts, vertical, TILE)
            new_maps, new_out = jax.vmap(partial(reorder_box, pieces=pieces))(new_maps, new_out)
        maps = new_maps.reshape(grid_shape + new_maps.shape[1:])
        outgoing = new_out.reshape(grid_shape + new_out.shape[1:])
    return (spread_rows(maps), spread_rows(outgoing))
```

```python
import jax
import jax.numpy as jnp
from jax import lax
from jax.experimental import pallas as pl
from jax.experimental.pallas import tpu as pltpu
from jax.sharding import PartitionSpec as P

F32 = jnp.float32
B16 = jnp.bfloat16
SQUARINGS = 8
SEG = 64
RHS = 128
WIRE = B16
VMEM_LIMIT = 24 * 1024 * 1024


def roles():
    row = lax.axis_index("tx")
    col = lax.axis_index("ty")
    even = (row & 1) == 0
    left = (col & 1) == 0
    inner = (((row + 1) >> 1) & 1) == 1
    upper = ((row >> 1) & 1) == 1
    return even, left, inner, upper


def side_order(even, left):
    return (
        jnp.where(even, 2, 0),
        jnp.where(left, 1, 3),
        jnp.where(even, 0, 2),
        jnp.where(left, 3, 1),
    )


def low_half(shape):
    return lax.broadcasted_iota(jnp.int32, shape, len(shape) - 1) % 128 < SEG


def half_roll(value):
    return jnp.concatenate([value[:, SEG:], value[:, :SEG]], axis=1)


def split(value):
    high = value.astype(B16)
    return high, (value - high.astype(F32)).astype(B16)


def times_i(stacked):
    half = stacked.shape[0] // 2
    return jnp.concatenate([-stacked[half:], stacked[:half]], axis=0)


def embed(stacked):
    return jnp.concatenate([stacked, times_i(stacked)], axis=1)


def dot(left, right):
    return jnp.dot(left, right, preferred_element_type=F32)


def dot_split(left, right):
    return dot(left[0], right[0]) + (dot(left[0], right[1]) + dot(left[1], right[0]))


def complex_dot(left, right):
    lefts = split(left)
    return dot_split((embed(lefts[0]), embed(lefts[1])), split(right))


def neumann(power):
    size = power.shape[1]
    rows = lax.broadcasted_iota(jnp.int32, power.shape, 0)
    cols = lax.broadcasted_iota(jnp.int32, power.shape, 1)
    total = power + jnp.where(rows == cols, 1.0, 0.0).astype(F32)
    power = complex_dot(power, power)
    for k in range(1, SQUARINGS):
        both = total
        if k + 1 < SQUARINGS:
            both = jnp.concatenate([power, total], axis=1)
        if k < 4:
            step = complex_dot(power, both)
        else:
            step = dot(embed(power.astype(B16)), both.astype(B16))
        if k + 1 < SQUARINGS:
            power = step[:, :size]
            step = step[:, size:]
        total = total + step
    return total


def stack(ref, begin, length):
    return jnp.concatenate([ref[0, begin : begin + length], ref[1, begin : begin + length]], axis=0).astype(F32)


def store_stacked(ref, value, begin=0):
    half = value.shape[0] // 2
    ref[0, begin : begin + half] = value[:half].astype(ref.dtype)
    ref[1, begin : begin + half] = value[half:].astype(ref.dtype)


def rows_of(stacked, begin, length):
    half = stacked.shape[0] // 2
    return jnp.concatenate(
        [stacked[begin : begin + length], stacked[half + begin : half + begin + length]], axis=0
    )


def join_rows(parts):
    halves = [p.shape[0] // 2 for p in parts]
    return jnp.concatenate(
        [p[:h] for p, h in zip(parts, halves)] + [p[h:] for p, h in zip(parts, halves)], axis=0
    )


def front_kernel(guess_ref, leaf_ref, row_i, row_k, col_j, col_l, own_ref, send_ref, leaf, sems):
    even, left, inner, _ = roles()
    row = jnp.where(even, SEG - 1, 0)
    col = jnp.where(left, SEG - 1, 0)
    copies = [
        pltpu.make_async_copy(guess_ref.at[row], row_i, sems.at[0]),
        pltpu.make_async_copy(guess_ref.at[SEG - 1 - row], row_k, sems.at[1]),
        pltpu.make_async_copy(guess_ref.at[:, col], col_j, sems.at[2]),
        pltpu.make_async_copy(guess_ref.at[:, SEG - 1 - col], col_l, sems.at[3]),
        pltpu.make_async_copy(leaf_ref, leaf, sems.at[4]),
    ]
    for copy in copies:
        copy.start()
    copies[4].wait()
    low = low_half((SEG, 128))
    crossed = (low & even) | (~low & ~left)
    for part in range(2):
        for place, side in enumerate(side_order(even, left)):
            rows = leaf[part, pl.ds(pl.multiple_of(side * SEG, SEG), SEG), :]
            first = rows[:, :128]
            second = rows[:, 128:]
            near = jnp.where(crossed, second, first)
            far = jnp.where(crossed, first, second)
            near = jnp.where(inner, half_roll(near), near)
            own_ref[part, place * SEG : (place + 1) * SEG, :128] = near
            own_ref[part, place * SEG : (place + 1) * SEG, 128:] = far
            if place < 3:
                send_ref[part, place * SEG : (place + 1) * SEG, :128] = near.astype(send_ref.dtype)
                send_ref[part, place * SEG : (place + 1) * SEG, 128:] = far.astype(send_ref.dtype)
    for copy in copies[:4]:
        copy.wait()


def planes_matrix(size=2 * SEG):
    row = lax.broadcasted_iota(jnp.int32, (size, size), 0)
    col = lax.broadcasted_iota(jnp.int32, (size, size), 1)
    return jnp.where(col == 2 * (row % SEG) + row // SEG, 1.0, 0.0).astype(B16)


def stencil_matrix():
    width = 2 * SEG
    row = lax.broadcasted_iota(jnp.int32, (width, width), 0)
    col = lax.broadcasted_iota(jnp.int32, (width, width), 1)
    apart = jnp.abs(col - 2 * (row % SEG) - row // SEG)
    own = jnp.where(apart == 0, 1.0, 0.0).astype(F32)
    beside = jnp.where(apart == 2, 1.0, 0.0).astype(F32)
    ahead = jnp.concatenate([own, beside - 4.0 * own], axis=1)
    value = jnp.concatenate([jnp.zeros_like(own), own], axis=1)
    return jnp.concatenate([ahead, value], axis=0).astype(B16)


BLOCK = 8
BLOCKS = SEG // BLOCK


def stencil_kernel(
    source_ref, guess_ref, coef_ref, body_ref, flat_ref, body_out, source, guess, coef_rows,
    source_sems, guess_sems, body_sems, coef_sem,
):
    width = 2 * SEG
    chunk = BLOCK * width
    span = BLOCK * SEG

    def source_copy(i):
        rows = pl.ds(i * chunk, chunk)
        return pltpu.make_async_copy(source_ref.at[rows], source.at[rows], source_sems.at[i])

    def guess_copy(i):
        rows = pl.ds(i * chunk, chunk)
        return pltpu.make_async_copy(guess_ref.at[rows], guess.at[rows], guess_sems.at[i])

    def body_copy(i):
        rows = pl.ds(i * SEG, SEG)
        return pltpu.make_async_copy(body_ref.at[rows], body_out.at[rows], body_sems.at[i])

    coef_copy = pltpu.make_async_copy(coef_ref, coef_rows, coef_sem)
    coef_copy.start()
    for i in range(BLOCKS):
        guess_copy(i).start()
        source_copy(i).start()
    for i in range(BLOCKS):
        body_copy(i).start()
    table = stencil_matrix()
    planes = planes_matrix()
    coef_copy.wait()
    guess_copy(0).wait()

    def block(i, carry):
        @pl.when(i + 1 < BLOCKS)
        def _():
            guess_copy(i + 1).wait()

        source_copy(i).wait()
        base = i * chunk

        def rows_at(ref, begin):
            return ref[pl.ds(pl.multiple_of(begin, width), width), :]

        below = rows_at(guess, jnp.maximum(base - width, 0))
        above = rows_at(guess, jnp.minimum(base + chunk, SEG * width - width))
        outer = dot(planes, jnp.concatenate([below, above], axis=1))
        values = {
            -1: jnp.where(i == 0, 0.0, outer[:, :RHS]),
            BLOCK: jnp.where(i == BLOCKS - 1, 0.0, outer[:, RHS:]),
        }
        ahead = {}
        for k in range(0, BLOCK, 2):
            pair = [
                jnp.concatenate([rows_at(source, base + r * width), rows_at(guess, base + r * width)], axis=0)
                for r in (k, k + 1)
            ]
            both = dot(table, jnp.concatenate(pair, axis=1))
            for j, r in enumerate((k, k + 1)):
                ahead[r] = both[:width, j * RHS : (j + 1) * RHS]
                values[r] = both[width:, j * RHS : (j + 1) * RHS]
        coef = coef_rows[pl.ds(pl.multiple_of(i * BLOCK, BLOCK), BLOCK), :].T
        for r in range(BLOCK):
            wave = jnp.broadcast_to(coef[:, r : r + 1], (SEG, RHS))
            sums = ahead[r] + (values[r - 1] + values[r + 1])
            real_part = values[r][:SEG]
            imag_part = values[r][SEG:]
            cells = pl.ds(pl.multiple_of(i * span + r * SEG, SEG), SEG)
            flat_ref[cells, :RHS] = sums[:SEG] + wave * (real_part - 0.5 * imag_part)
            flat_ref[cells, RHS:] = sums[SEG:] + wave * (imag_part + 0.5 * real_part)
        return carry

    lax.fori_loop(0, BLOCKS, block, 0)
    for i in range(BLOCKS):
        body_copy(i).wait()


def leaf_kernel(
    flat_ref, body_ref, across_i, across_j, across_k, across_l, own_ref, send_ref, total, west_ref, east_ref
):
    even, left, _, _ = roles()
    at_row = lax.axis_index("tx")
    at_col = lax.axis_index("ty")
    strips = dot(planes_matrix(), jnp.concatenate([across_i[...], across_k[...]], axis=1))
    south = jnp.where(even, strips[:, RHS:], strips[:, :RHS])
    north = jnp.where(even, strips[:, :RHS], strips[:, RHS:])
    south = jnp.where(at_row == 0, 0.0, south)
    north = jnp.where(at_row == lax.axis_size("tx") - 1, 0.0, north)
    near = across_j[...].astype(F32)
    far = across_l[...].astype(F32)
    west_ref[...] = jnp.where(at_col == 0, 0.0, jnp.where(left, far, near))
    east_ref[...] = jnp.where(at_col == lax.axis_size("ty") - 1, 0.0, jnp.where(left, near, far))
    row8 = lax.broadcasted_iota(jnp.int32, (8, RHS), 0)
    span = BLOCK * SEG

    def block(i):
        cells = []
        for r in range(BLOCK):
            parts = []
            for c in range(2):
                rows = pl.ds(pl.multiple_of(i * span + r * SEG, SEG), SEG)
                flat = flat_ref[rows, c * RHS : (c + 1) * RHS]
                if r == 0:
                    flat = flat + jnp.where(i == 0, south[c * SEG : (c + 1) * SEG], 0.0)
                if r == BLOCK - 1:
                    flat = flat + jnp.where(i == BLOCKS - 1, north[c * SEG : (c + 1) * SEG], 0.0)
                at = 2 * (i * BLOCK + r) + c
                begin = flat[:8] + jnp.where(row8 == 0, west_ref[pl.ds(at, 1), :], 0.0)
                end = flat[SEG - 8 :] + jnp.where(row8 == 7, east_ref[pl.ds(at, 1), :], 0.0)
                parts.append(jnp.concatenate([begin, flat[8 : SEG - 8], end], axis=0).astype(B16))
            cells.append(jnp.concatenate(parts, axis=1))
        return dot(body_ref[:, pl.ds(pl.multiple_of(i * span, span), span)], jnp.concatenate(cells, axis=0))

    total[...] = block(0)

    def add(i, carry):
        total[...] += block(i)
        return carry

    lax.fori_loop(1, BLOCKS, add, 0)
    half = total.shape[0] // 2
    real_part = total[:half, :RHS] - total[half:, RHS:]
    imag_part = total[:half, RHS:] + total[half:, :RHS]
    total[:half, :RHS] = real_part
    total[half:, :RHS] = imag_part
    for part in range(2):
        for place, side in enumerate(side_order(even, left)):
            rows = total[pl.ds(pl.multiple_of(part * half + side * SEG, SEG), SEG), :RHS]
            own_ref[part, place * SEG : (place + 1) * SEG] = rows
            if place < 3:
                send_ref[part, place * SEG : (place + 1) * SEG] = rows.astype(send_ref.dtype)


def merge_rows_kernel(own_ref, partner_ref, face_ref, keep_ref, gain_ref):
    _, _, inner, _ = roles()

    def pick(place):
        mine = stack(own_ref, place * SEG, SEG)
        theirs = stack(partner_ref, place * SEG, SEG)
        return jnp.where(inner, mine, theirs), jnp.where(inner, theirs, mine)

    n_i, u_i = pick(0)
    n_j, u_j = pick(1)
    n_k, _ = pick(2)
    out = jnp.where(inner, stack(own_ref, 3 * SEG, SEG), stack(own_ref, 2 * SEG, SEG))
    inner_n = n_i[:, SEG:128]
    inner_u = u_i[:, :SEG]
    inverse = neumann(complex_dot(inner_u, inner_n))
    into_n = jnp.concatenate([complex_dot(inverse, inner_u), -inverse], axis=1)
    rows = lax.broadcasted_iota(jnp.int32, (128, 128), 0)
    cols = lax.broadcasted_iota(jnp.int32, (128, 128), 1)
    unit = jnp.where((rows == cols) & (cols < SEG), 1.0, 0.0).astype(F32)
    into_u = -unit - complex_dot(inner_n, into_n)
    gain_n = complex_dot(join_rows([n_j[:, SEG:128], n_k[:, SEG:128]]), into_n)
    gain_u = complex_dot(u_j[:, :SEG], into_u)
    gain_out = complex_dot(
        jnp.where(inner, out[:, SEG:128], out[:, :SEG]), jnp.where(inner, into_n, into_u)
    )
    gain = join_rows([rows_of(gain_n, 0, SEG), gain_u, rows_of(gain_n, SEG, SEG), gain_out])
    store_stacked(gain_ref, gain)
    zero = jnp.zeros_like(n_j)
    in_n = complex_dot(gain[:, :SEG], n_i) + join_rows([n_j, zero, n_k, jnp.where(inner, out, 0.0)])
    in_u = complex_dot(gain[:, SEG:], u_i) + join_rows([zero, u_j, zero, jnp.where(inner, 0.0, out)])
    joint = jnp.where(low_half((512, 128)), in_n[:, :128], in_u[:, :128])
    merged = jnp.concatenate([joint, in_n[:, 128:], in_u[:, 128:]], axis=1)
    store_stacked(face_ref, rows_of(merged, 0, 128))
    store_stacked(keep_ref, rows_of(merged, 128, 128))


def load_rows_kernel(own_ref, partner_ref, gain_ref, face_ref, keep_ref):
    _, _, inner, _ = roles()

    def pick(place):
        mine = stack(own_ref, place * SEG, SEG)
        theirs = stack(partner_ref, place * SEG, SEG)
        return jnp.where(inner, mine, theirs), jnp.where(inner, theirs, mine)

    n_i, u_i = pick(0)
    n_j, u_j = pick(1)
    n_k, _ = pick(2)
    out = jnp.where(inner, stack(own_ref, 3 * SEG, SEG), stack(own_ref, 2 * SEG, SEG))
    merged = complex_dot(stack(gain_ref, 0, 256), join_rows([n_i, u_i])) + join_rows([n_j, u_j, n_k, out])
    store_stacked(face_ref, rows_of(merged, 0, 128))
    store_stacked(keep_ref, rows_of(merged, 128, 128))


def merge_cols_kernel(own_ref, across_ref, keep_ref, face_ref, send_ref, out_ref, gain_ref):
    _, left, _, upper = roles()
    own = stack(own_ref, 0, 128)
    across = stack(across_ref, 0, 128)
    keep = stack(keep_ref, 0, 128)
    inverse = neumann(complex_dot(across[:, :128], own[:, :128]))
    bounced = complex_dot(across[:, :128], own[:, 128:])
    carried = complex_dot(keep[:, :128], inverse)
    gained = complex_dot(carried, jnp.concatenate([bounced, across], axis=1))
    store_stacked(gain_ref, jnp.concatenate([gained[:, 256:384], -carried], axis=1))
    mine = keep[:, 128:] + gained[:, :256]
    theirs = -gained[:, 384:]
    west = jnp.where(left, mine, theirs)
    east = jnp.where(left, theirs, mine)
    low = low_half((256, 128))
    west_n, west_u = west[:, :128], west[:, 128:]
    east_n, east_u = east[:, :128], east[:, 128:]
    roll_wn, roll_wu, roll_en, roll_eu = [half_roll(v) for v in (west_n, west_u, east_n, east_u)]
    inner_k = jnp.where(low, west_n, roll_en)
    outer_k = jnp.where(low, west_u, roll_eu)
    east_l = jnp.where(upper, jnp.where(low, roll_en, east_u), jnp.where(low, roll_eu, east_n))
    west_l = jnp.where(upper, jnp.where(low, roll_wn, west_u), jnp.where(low, roll_wu, west_n))
    merged = jnp.concatenate([inner_k, outer_k, east_l, west_l], axis=1)
    face = rows_of(merged, 0, SEG)
    store_stacked(face_ref, face)
    store_stacked(send_ref, face)
    store_stacked(out_ref, rows_of(merged, SEG, SEG))


def load_cols_kernel(own_ref, across_ref, keep_ref, gain_ref, face_ref, send_ref, out_ref):
    sides = join_rows([stack(own_ref, 0, 128), stack(across_ref, 0, 128)])
    merged = stack(keep_ref, 0, 128) + complex_dot(stack(gain_ref, 0, 128), sides)
    face = rows_of(merged, 0, SEG)
    store_stacked(face_ref, face)
    store_stacked(send_ref, face)
    store_stacked(out_ref, rows_of(merged, SEG, SEG))


def top_kernel(
    own_ref, mate_ref, far_ref, far_mate_ref, out_ref,
    own_load, mate_load, far_load, far_mate_load, out_load, map_ref, load_ref,
):
    _, left, _, upper = roles()

    def both(mine_ref, theirs_ref):
        mine = stack(mine_ref, 0, SEG)
        theirs = stack(theirs_ref, 0, SEG)
        return join_rows([jnp.where(left, mine, theirs), jnp.where(left, theirs, mine)])

    near = both(own_ref, mate_ref)
    far = both(far_ref, far_mate_ref)
    rows = stack(out_ref, 0, SEG)
    inverse = neumann(complex_dot(far[:, :128], near[:, :128]))
    near_load = both(own_load, mate_load)
    far_load_rows = both(far_load, far_mate_load)
    bounced = complex_dot(far[:, :128], jnp.concatenate([near[:, 128:], near_load], axis=1))
    carried = complex_dot(rows[:, :128], inverse)
    gained = complex_dot(carried, jnp.concatenate([bounced, far[:, 128:], far_load_rows], axis=1))
    mine = rows[:, 128:] + gained[:, :384]
    theirs = -gained[:, 512:896]
    store_stacked(load_ref, stack(out_load, 0, SEG) + gained[:, 384:512] - gained[:, 896:])
    lower_part = jnp.where(upper, theirs, mine)
    upper_part = jnp.where(upper, mine, theirs)
    store_stacked(
        map_ref,
        jnp.concatenate(
            [lower_part, upper_part[:, 128:256], upper_part[:, :128], upper_part[:, 256:]], axis=1
        ),
    )


def call(kernel, name, outs, *args, kept=0, scratch=()):
    args = [pltpu.with_memory_space_constraint(v, pltpu.HBM) if i < kept else v for i, v in enumerate(args)]
    return pl.pallas_call(
        kernel,
        in_specs=[pl.BlockSpec(memory_space=pltpu.HBM if i < kept else pltpu.VMEM) for i in range(len(args))],
        out_shape=[jax.ShapeDtypeStruct(shape, dtype) for shape, dtype in outs],
        scratch_shapes=list(scratch),
        compiler_params=pltpu.CompilerParams(vmem_limit_bytes=VMEM_LIMIT),
        name=name,
    )(*args)


def swap_near(value, axis):
    return lax.ppermute(value, axis, [(i, i ^ 1) for i in range(lax.axis_size(axis))])


def swap_far(value, axis):
    count = lax.axis_size(axis)
    pairs = []
    for i in range(1, count, 2):
        pairs += [(i, (i + 1) % count), ((i + 1) % count, i)]
    return lax.ppermute(value, axis, pairs)


def from_other_half(value):
    return lax.ppermute(value, "tx", [(i, i ^ 3) for i in range(lax.axis_size("tx"))])


def on_device(source, guess, coefficient, leaf_map, body_map):
    dma = pltpu.SemaphoreType.DMA
    strip = ((SEG, 2, RHS), B16)
    *strips, own, sent = call(
        front_kernel, "front",
        [strip, strip, strip, strip, ((2, 256, 256), F32), ((2, 192, 256), WIRE)],
        guess, leaf_map[0, 0], kept=2, scratch=[pltpu.VMEM((2, 256, 256), F32), dma((5,))],
    )
    row_i, row_k, col_j, col_l = [strip.reshape(128, RHS) for strip in strips]
    across_k = swap_far(row_k, "tx")
    across_l = swap_far(col_l, "ty")
    across_i = swap_near(row_i, "tx")
    across_j = swap_near(col_j, "ty")
    partner = swap_near(sent, "tx")
    flat, body = call(
        stencil_kernel, "stencil",
        [((SEG * SEG, 2 * RHS), F32), ((512, SEG * SEG), B16)],
        source.reshape(SEG * SEG * 2, RHS), guess.reshape(SEG * SEG * 2, RHS), coefficient,
        body_map.reshape(512, SEG * SEG), kept=4,
        scratch=[
            pltpu.VMEM((SEG * SEG * 2, RHS), B16), pltpu.VMEM((SEG * SEG * 2, RHS), B16),
            pltpu.VMEM((SEG, SEG), F32), dma((BLOCKS,)), dma((BLOCKS,)), dma((BLOCKS,)), dma(()),
        ],
    )
    own_load, sent_load = call(
        leaf_kernel, "leaf_loads", [((2, 256, RHS), F32), ((2, 192, RHS), WIRE)],
        flat, body, across_i, across_j, across_k, across_l,
        scratch=[pltpu.VMEM((512, 2 * RHS), F32), pltpu.VMEM((128, RHS), F32), pltpu.VMEM((128, RHS), F32)],
    )
    partner, sent_load = lax.optimization_barrier((partner, sent_load))
    partner_load = swap_near(sent_load, "tx")

    face1, keep1, gain1 = call(
        merge_rows_kernel, "merge_rows",
        [((2, 128, 384), F32), ((2, 128, 384), F32), ((2, 256, 128), F32)], own, partner,
    )
    face1_across = swap_near(face1, "ty")
    face2, send2, out2, gain2 = call(
        merge_cols_kernel, "merge_cols",
        [((2, 64, 512), F32), ((2, 64, 512), WIRE), ((2, 64, 512), F32), ((2, 128, 256), F32)],
        face1, face1_across, keep1,
    )
    face2_far = from_other_half(send2)
    face2_mate = swap_near(face2, "ty")

    load1, keep_load1 = call(
        load_rows_kernel, "load_rows", [((2, 128, RHS), F32)] * 2, own_load, partner_load, gain1
    )
    load1_across = swap_near(load1, "ty")
    load2, send_load2, out_load2 = call(
        load_cols_kernel, "load_cols",
        [((2, 64, RHS), F32), ((2, 64, RHS), WIRE), ((2, 64, RHS), F32)],
        load1, load1_across, keep_load1, gain2,
    )
    load2_far = from_other_half(send_load2)
    load2_mate = swap_near(load2, "ty")
    far_mate = swap_near(face2_far, "ty")
    load_far_mate = swap_near(load2_far, "ty")
    top_map, top_out = call(
        top_kernel, "merge_top", [((2, 64, 768), F32), ((2, 64, RHS), F32)],
        face2, face2_mate, face2_far, far_mate, out2,
        load2, load2_mate, load2_far, load_far_mate, out_load2,
    )
    return top_map[None, None], top_out[None, None]


def solution(mesh):
    placed = (
        P("tx", "ty", None, None),
        P("tx", "ty", None, None),
        P("tx", "ty"),
        P("tx", "ty", None, None, None),
        P("tx", "ty", None, None, None),
    )
    return jax.shard_map(
        on_device,
        mesh=mesh,
        in_specs=placed,
        out_specs=(P("tx", "ty", None, None, None), P("tx", "ty", None, None, None)),
        check_vma=False,
    )
```

```python
import jax
import jax.numpy as jnp
from jax import lax
from jax.experimental import pallas as pl
from jax.experimental.pallas import tpu as pltpu
from jax.sharding import PartitionSpec as P

F32 = jnp.float32
B16 = jnp.bfloat16
SQUARINGS = 8
SEG = 64
RHS = 128
WIRE = B16
VMEM_LIMIT = 24 * 1024 * 1024


def roles():
    row = lax.axis_index("tx")
    col = lax.axis_index("ty")
    even = (row & 1) == 0
    left = (col & 1) == 0
    inner = (((row + 1) >> 1) & 1) == 1
    upper = ((row >> 1) & 1) == 1
    return even, left, inner, upper


def side_order(even, left):
    return (
        jnp.where(even, 2, 0),
        jnp.where(left, 1, 3),
        jnp.where(even, 0, 2),
        jnp.where(left, 3, 1),
    )


def low_half(shape):
    return lax.broadcasted_iota(jnp.int32, shape, len(shape) - 1) % 128 < SEG


def half_roll(value):
    return jnp.concatenate([value[:, SEG:], value[:, :SEG]], axis=1)


def split(value):
    high = value.astype(B16)
    return high, (value - high.astype(F32)).astype(B16)


def times_i(stacked):
    half = stacked.shape[0] // 2
    return jnp.concatenate([-stacked[half:], stacked[:half]], axis=0)


def embed(stacked):
    return jnp.concatenate([stacked, times_i(stacked)], axis=1)


def dot(left, right):
    return jnp.dot(left, right, preferred_element_type=F32)


def dot_split(left, right):
    return dot(left[0], right[0]) + (dot(left[0], right[1]) + dot(left[1], right[0]))


def complex_dot(left, right):
    lefts = split(left)
    return dot_split((embed(lefts[0]), embed(lefts[1])), split(right))


def neumann_small(power):
    power = embed(power)
    rows = lax.broadcasted_iota(jnp.int32, power.shape, 0)
    cols = lax.broadcasted_iota(jnp.int32, power.shape, 1)
    total = power + jnp.where(rows == cols, 1.0, 0.0).astype(F32)
    parts = split(power)
    power = dot_split(parts, parts)
    for k in range(1, SQUARINGS):
        last = k + 1 == SQUARINGS
        both = total if last else jnp.concatenate([power, total], axis=1)
        if k < 3:
            step = dot_split(split(power), split(both))
        else:
            step = dot(power.astype(B16), both.astype(B16))
        if not last:
            power = step[:, :128]
            step = step[:, 128:]
        total = total + step
    return total


def neumann(power):
    size = power.shape[1]
    rows = lax.broadcasted_iota(jnp.int32, power.shape, 0)
    cols = lax.broadcasted_iota(jnp.int32, power.shape, 1)
    total = power + jnp.where(rows == cols, 1.0, 0.0).astype(F32)
    power = complex_dot(power, power)
    for k in range(1, SQUARINGS):
        both = total
        if k + 1 < SQUARINGS:
            both = jnp.concatenate([power, total], axis=1)
        if k < 3:
            step = complex_dot(power, both)
        else:
            step = dot(embed(power.astype(B16)), both.astype(B16))
        if k + 1 < SQUARINGS:
            power = step[:, :size]
            step = step[:, size:]
        total = total + step
    return total


def stack(ref, begin, length):
    return jnp.concatenate([ref[0, begin : begin + length], ref[1, begin : begin + length]], axis=0).astype(F32)


def store_stacked(ref, value, begin=0):
    half = value.shape[0] // 2
    ref[0, begin : begin + half] = value[:half].astype(ref.dtype)
    ref[1, begin : begin + half] = value[half:].astype(ref.dtype)


def rows_of(stacked, begin, length):
    half = stacked.shape[0] // 2
    return jnp.concatenate(
        [stacked[begin : begin + length], stacked[half + begin : half + begin + length]], axis=0
    )


def join_rows(parts):
    halves = [p.shape[0] // 2 for p in parts]
    return jnp.concatenate(
        [p[:h] for p, h in zip(parts, halves)] + [p[h:] for p, h in zip(parts, halves)], axis=0
    )


STRIP = 12 * SEG


def front_kernel(guess_ref, cells_ref, leaf_ref, row_k, col_j, col_l, own_ref, send_ref, leaf, sems):
    even, left, inner, _ = roles()
    row = jnp.where(even, SEG - 1, 0)
    col = jnp.where(left, SEG - 1, 0)
    copies = [
        pltpu.make_async_copy(
            cells_ref.at[pl.ds(pl.multiple_of(row * 128, 128), 128)], send_ref.at[pl.ds(STRIP, 128)], sems.at[0]
        ),
        pltpu.make_async_copy(guess_ref.at[SEG - 1 - row], row_k, sems.at[1]),
        pltpu.make_async_copy(guess_ref.at[:, col], col_j, sems.at[2]),
        pltpu.make_async_copy(guess_ref.at[:, SEG - 1 - col], col_l, sems.at[3]),
        pltpu.make_async_copy(leaf_ref, leaf, sems.at[4]),
    ]
    for copy in copies:
        copy.start()
    copies[4].wait()
    low = low_half((SEG, 128))
    crossed = (low & even) | (~low & ~left)
    for part in range(2):
        for place, side in enumerate(side_order(even, left)):
            rows = leaf[part, pl.ds(pl.multiple_of(side * SEG, SEG), SEG), :]
            first = rows[:, :128]
            second = rows[:, 128:]
            near = jnp.where(crossed, second, first)
            far = jnp.where(crossed, first, second)
            near = jnp.where(inner, half_roll(near), near)
            own_ref[part, place * SEG : (place + 1) * SEG, :128] = near
            own_ref[part, place * SEG : (place + 1) * SEG, 128:] = far
            if place < 3:
                at = (part * 3 + place) * 2 * SEG
                send_ref[at : at + SEG] = near.astype(send_ref.dtype)
                send_ref[at + SEG : at + 2 * SEG] = far.astype(send_ref.dtype)
    for copy in copies[:4]:
        copy.wait()


def planes_matrix(size=2 * SEG):
    row = lax.broadcasted_iota(jnp.int32, (size, size), 0)
    col = lax.broadcasted_iota(jnp.int32, (size, size), 1)
    return jnp.where(col == 2 * (row % SEG) + row // SEG, 1.0, 0.0).astype(B16)


def stencil_matrix():
    width = 2 * SEG
    row = lax.broadcasted_iota(jnp.int32, (width, width), 0)
    col = lax.broadcasted_iota(jnp.int32, (width, width), 1)
    apart = jnp.abs(col - 2 * (row % SEG) - row // SEG)
    own = jnp.where(apart == 0, 1.0, 0.0).astype(F32)
    beside = jnp.where(apart == 2, 1.0, 0.0).astype(F32)
    ahead = jnp.concatenate([own, beside - 4.0 * own], axis=1)
    value = jnp.concatenate([jnp.zeros_like(own), own], axis=1)
    return jnp.concatenate([ahead, value], axis=0).astype(B16)


COSTS = (5.0, 3.0, 0.4, 0.8, 3.0)
BLOCK = 16
BLOCKS = SEG // BLOCK
AHEAD = 3


def stencil_kernel(
    source_ref, guess_ref, coef_ref, body_ref, flat_ref, body_out, source, guess, coef_rows,
    source_sems, guess_sems, body_sems, coef_sem,
):
    width = 2 * SEG
    chunk = BLOCK * width
    span = BLOCK * SEG

    def source_copy(i):
        rows = pl.ds(i * chunk, chunk)
        return pltpu.make_async_copy(source_ref.at[rows], source.at[rows], source_sems.at[i])

    def guess_copy(i):
        rows = pl.ds(i * chunk, chunk)
        return pltpu.make_async_copy(guess_ref.at[rows], guess.at[rows], guess_sems.at[i])

    def body_copy(i):
        rows = pl.ds(i * (512 // BLOCKS), 512 // BLOCKS)
        return pltpu.make_async_copy(body_ref.at[rows], body_out.at[rows], body_sems.at[i])

    coef_copy = pltpu.make_async_copy(coef_ref, coef_rows, coef_sem)
    coef_copy.start()
    for i in range(AHEAD):
        guess_copy(i).start()
        source_copy(i).start()
    table = stencil_matrix()
    planes = planes_matrix()
    coef_copy.wait()
    guess_copy(0).wait()

    def block(i, carry):
        @pl.when(i + AHEAD < BLOCKS)
        def _():
            guess_copy(i + AHEAD).start()
            source_copy(i + AHEAD).start()

        body_copy(i).start()

        @pl.when(i + 1 < BLOCKS)
        def _():
            guess_copy(i + 1).wait()

        source_copy(i).wait()
        base = i * chunk

        def rows_at(ref, begin):
            return ref[pl.ds(pl.multiple_of(begin, width), width), :]

        below = rows_at(guess, jnp.maximum(base - width, 0))
        above = rows_at(guess, jnp.minimum(base + chunk, SEG * width - width))
        outer = dot(planes, jnp.concatenate([below, above], axis=1))
        values = {
            -1: jnp.where(i == 0, 0.0, outer[:, :RHS]),
            BLOCK: jnp.where(i == BLOCKS - 1, 0.0, outer[:, RHS:]),
        }
        ahead = {}
        coef = coef_rows[pl.ds(pl.multiple_of(i * BLOCK, BLOCK), BLOCK), :].T

        def finish(r):
            wave = jnp.broadcast_to(coef[:, r : r + 1], (SEG, RHS))
            sums = ahead[r] + (values[r - 1] + values[r + 1])
            real_part = values[r][:SEG]
            imag_part = values[r][SEG:]
            cells = pl.ds(pl.multiple_of(i * span + r * SEG, SEG), SEG)
            flat_ref[cells, :RHS] = sums[:SEG] + wave * (real_part - 0.5 * imag_part)
            flat_ref[cells, RHS:] = sums[SEG:] + wave * (imag_part + 0.5 * real_part)

        for k in range(0, BLOCK, 2):
            pair = [
                jnp.concatenate([rows_at(source, base + r * width), rows_at(guess, base + r * width)], axis=0)
                for r in (k, k + 1)
            ]
            both = dot(table, jnp.concatenate(pair, axis=1))
            for j, r in enumerate((k, k + 1)):
                ahead[r] = both[:width, j * RHS : (j + 1) * RHS]
                values[r] = both[width:, j * RHS : (j + 1) * RHS]
            if k > 0:
                finish(k - 1)
            finish(k)
        finish(BLOCK - 1)
        return carry

    lax.fori_loop(0, BLOCKS, block, 0)
    for i in range(BLOCKS):
        body_copy(i).wait()


def leaf_kernel(
    flat_ref, body_ref, across_j, across_k, across_l, partner_ref, own_ref, send_ref, total, west_ref, east_ref
):
    even, left, _, _ = roles()
    at_row = lax.axis_index("tx")
    at_col = lax.axis_index("ty")
    strips = dot(planes_matrix(), jnp.concatenate([partner_ref[STRIP:], across_k[...]], axis=1))
    south = jnp.where(even, strips[:, RHS:], strips[:, :RHS])
    north = jnp.where(even, strips[:, :RHS], strips[:, RHS:])
    south = jnp.where(at_row == 0, 0.0, south)
    north = jnp.where(at_row == lax.axis_size("tx") - 1, 0.0, north)
    near = across_j[...].astype(F32)
    far = across_l[...].astype(F32)
    west_ref[...] = jnp.where(at_col == 0, 0.0, jnp.where(left, far, near))
    east_ref[...] = jnp.where(at_col == lax.axis_size("ty") - 1, 0.0, jnp.where(left, near, far))
    row8 = lax.broadcasted_iota(jnp.int32, (8, RHS), 0)
    span = BLOCK * SEG

    def block(i):
        cells = []
        for r in range(BLOCK):
            parts = []
            for c in range(2):
                rows = pl.ds(pl.multiple_of(i * span + r * SEG, SEG), SEG)
                flat = flat_ref[rows, c * RHS : (c + 1) * RHS]
                if r == 0:
                    flat = flat + jnp.where(i == 0, south[c * SEG : (c + 1) * SEG], 0.0)
                if r == BLOCK - 1:
                    flat = flat + jnp.where(i == BLOCKS - 1, north[c * SEG : (c + 1) * SEG], 0.0)
                at = 2 * (i * BLOCK + r) + c
                begin = flat[:8] + jnp.where(row8 == 0, west_ref[pl.ds(at, 1), :], 0.0)
                end = flat[SEG - 8 :] + jnp.where(row8 == 7, east_ref[pl.ds(at, 1), :], 0.0)
                parts.append(jnp.concatenate([begin, flat[8 : SEG - 8], end], axis=0).astype(B16))
            cells.append(jnp.concatenate(parts, axis=1))
        return dot(body_ref[:, pl.ds(pl.multiple_of(i * span, span), span)], jnp.concatenate(cells, axis=0))

    total[...] = block(0)

    def add(i, carry):
        total[...] += block(i)
        return carry

    lax.fori_loop(1, BLOCKS, add, 0)
    half = total.shape[0] // 2
    real_part = total[:half, :RHS] - total[half:, RHS:]
    imag_part = total[:half, RHS:] + total[half:, :RHS]
    total[:half, :RHS] = real_part
    total[half:, :RHS] = imag_part
    for part in range(2):
        for place, side in enumerate(side_order(even, left)):
            rows = total[pl.ds(pl.multiple_of(part * half + side * SEG, SEG), SEG), :RHS]
            own_ref[part, place * SEG : (place + 1) * SEG] = rows
            if place < 3:
                send_ref[part, place * SEG : (place + 1) * SEG] = rows.astype(send_ref.dtype)


def merge_rows_kernel(own_ref, partner_ref, face_ref, keep_ref, gain_ref):
    _, _, inner, _ = roles()

    def sent(place, part):
        at = (part * 3 + place) * 2 * SEG
        return jnp.concatenate([partner_ref[at : at + SEG], partner_ref[at + SEG : at + 2 * SEG]], axis=1)

    def pick(place):
        mine = stack(own_ref, place * SEG, SEG)
        theirs = jnp.concatenate([sent(place, 0), sent(place, 1)], axis=0).astype(F32)
        return jnp.where(inner, mine, theirs), jnp.where(inner, theirs, mine)

    n_i, u_i = pick(0)
    n_j, u_j = pick(1)
    n_k, _ = pick(2)
    out = jnp.where(inner, stack(own_ref, 3 * SEG, SEG), stack(own_ref, 2 * SEG, SEG))
    inner_n = n_i[:, SEG:128]
    inner_u = u_i[:, :SEG]
    solved = neumann_small(complex_dot(inner_u, inner_n))
    carried = dot_split(split(solved), split(inner_u))
    into_n = jnp.concatenate([carried, -solved[:, :SEG]], axis=1)
    rows = lax.broadcasted_iota(jnp.int32, (128, 128), 0)
    cols = lax.broadcasted_iota(jnp.int32, (128, 128), 1)
    unit = jnp.where((rows == cols) & (cols < SEG), 1.0, 0.0).astype(F32)
    into_u = -unit - complex_dot(inner_n, into_n)
    gain_n = complex_dot(join_rows([n_j[:, SEG:128], n_k[:, SEG:128]]), into_n)
    gain_u = complex_dot(u_j[:, :SEG], into_u)
    gain_out = complex_dot(
        jnp.where(inner, out[:, SEG:128], out[:, :SEG]), jnp.where(inner, into_n, into_u)
    )
    gain = join_rows([rows_of(gain_n, 0, SEG), gain_u, rows_of(gain_n, SEG, SEG), gain_out])
    store_stacked(gain_ref, gain)
    zero = jnp.zeros_like(n_j)
    in_n = complex_dot(gain[:, :SEG], n_i) + join_rows([n_j, zero, n_k, jnp.where(inner, out, 0.0)])
    in_u = complex_dot(gain[:, SEG:], u_i) + join_rows([zero, u_j, zero, jnp.where(inner, 0.0, out)])
    joint = jnp.where(low_half((512, 128)), in_n[:, :128], in_u[:, :128])
    merged = jnp.concatenate([joint, in_n[:, 128:], in_u[:, 128:]], axis=1)
    store_stacked(face_ref, rows_of(merged, 0, 128))
    store_stacked(keep_ref, rows_of(merged, 128, 128))


def load_rows_kernel(own_ref, partner_ref, gain_ref, face_ref, keep_ref):
    _, _, inner, _ = roles()

    def pick(place):
        mine = stack(own_ref, place * SEG, SEG)
        theirs = stack(partner_ref, place * SEG, SEG)
        return jnp.where(inner, mine, theirs), jnp.where(inner, theirs, mine)

    n_i, u_i = pick(0)
    n_j, u_j = pick(1)
    n_k, _ = pick(2)
    out = jnp.where(inner, stack(own_ref, 3 * SEG, SEG), stack(own_ref, 2 * SEG, SEG))
    merged = complex_dot(stack(gain_ref, 0, 256), join_rows([n_i, u_i])) + join_rows([n_j, u_j, n_k, out])
    store_stacked(face_ref, rows_of(merged, 0, 128))
    store_stacked(keep_ref, rows_of(merged, 128, 128))


def merge_cols_kernel(own_ref, across_ref, keep_ref, face_ref, send_near, out_ref, gain_ref):
    _, left, _, upper = roles()
    own = stack(own_ref, 0, 128)
    across = stack(across_ref, 0, 128)
    keep = stack(keep_ref, 0, 128)
    inverse = neumann(complex_dot(across[:, :128], own[:, :128]))
    bounced = complex_dot(across[:, :128], own[:, 128:])
    carried = complex_dot(keep[:, :128], inverse)
    gained = complex_dot(carried, jnp.concatenate([bounced, across], axis=1))
    store_stacked(gain_ref, jnp.concatenate([gained[:, 256:384], -carried], axis=1))
    mine = keep[:, 128:] + gained[:, :256]
    theirs = -gained[:, 384:]
    west = jnp.where(left, mine, theirs)
    east = jnp.where(left, theirs, mine)
    low = low_half((256, 128))
    west_n, west_u = west[:, :128], west[:, 128:]
    east_n, east_u = east[:, :128], east[:, 128:]
    roll_wn, roll_wu, roll_en, roll_eu = [half_roll(v) for v in (west_n, west_u, east_n, east_u)]
    inner_k = jnp.where(low, west_n, roll_en)
    outer_k = jnp.where(low, west_u, roll_eu)
    east_l = jnp.where(upper, jnp.where(low, roll_en, east_u), jnp.where(low, roll_eu, east_n))
    west_l = jnp.where(upper, jnp.where(low, roll_wn, west_u), jnp.where(low, roll_wu, west_n))
    merged = jnp.concatenate([inner_k, outer_k, east_l, west_l], axis=1)
    face = rows_of(merged, 0, SEG)
    store_stacked(face_ref, face)
    store_stacked(send_near, face[:, :128])
    store_stacked(out_ref, rows_of(merged, SEG, SEG))


def load_cols_kernel(own_ref, across_ref, keep_ref, gain_ref, map_ref, out_map, face_ref, send_ref, out_ref):
    sides = join_rows([stack(own_ref, 0, 128), stack(across_ref, 0, 128)])
    merged = stack(keep_ref, 0, 128) + complex_dot(stack(gain_ref, 0, 128), sides)
    for half in range(2):
        face_ref[half, :, :512] = map_ref[half]
        face_ref[half, :, 512:] = merged[half * 128 : half * 128 + SEG]
        send_ref[half, :, :384] = map_ref[half, :, 128:].astype(send_ref.dtype)
        send_ref[half, :, 384:] = merged[half * 128 : half * 128 + SEG].astype(send_ref.dtype)
        out_ref[half, :, :512] = out_map[half]
        out_ref[half, :, 512:] = merged[half * 128 + SEG : half * 128 + 128]


def sides_of(mine_ref, theirs_ref):
    _, left, _, _ = roles()
    mine = stack(mine_ref, 0, SEG)
    theirs = stack(theirs_ref, 0, SEG)
    return join_rows([jnp.where(left, mine, theirs), jnp.where(left, theirs, mine)])


def top_solve_kernel(own_ref, mate_ref, far_ref, far_mate_ref, out_ref, carried_ref, mine_ref):
    near = sides_of(own_ref, mate_ref)
    far = sides_of(far_ref, far_mate_ref)
    rows = stack(out_ref, 0, SEG)
    inverse = neumann(complex_dot(far, near[:, :128]))
    bounced = complex_dot(far, near[:, 128:])
    carried = complex_dot(rows[:, :128], inverse)
    store_stacked(carried_ref, carried)
    store_stacked(mine_ref, rows[:, 128:] + complex_dot(carried, bounced))


def top_kernel(carried_ref, mine_ref, far_ref, far_mate_ref, map_ref, load_ref):
    _, _, _, upper = roles()
    far = sides_of(far_ref, far_mate_ref).astype(B16)
    mine = stack(mine_ref, 0, SEG)
    lefts = split(stack(carried_ref, 0, SEG))
    theirs = -(dot(embed(lefts[0]), far) + dot(embed(lefts[1]), far))
    store_stacked(load_ref, mine[:, 384:] + theirs[:, 384:])
    lower_part = jnp.where(upper, theirs[:, :384], mine[:, :384])
    upper_part = jnp.where(upper, mine[:, :384], theirs[:, :384])
    store_stacked(
        map_ref,
        jnp.concatenate(
            [lower_part, upper_part[:, 128:256], upper_part[:, :128], upper_part[:, 256:]], axis=1
        ),
    )


def call(kernel, name, outs, *args, kept=0, scratch=(), cost=1.0):
    args = [pltpu.with_memory_space_constraint(v, pltpu.HBM) if i < kept else v for i, v in enumerate(args)]
    return pl.pallas_call(
        kernel,
        in_specs=[pl.BlockSpec(memory_space=pltpu.HBM if i < kept else pltpu.VMEM) for i in range(len(args))],
        out_shape=[jax.ShapeDtypeStruct(shape, dtype) for shape, dtype in outs],
        scratch_shapes=list(scratch),
        compiler_params=pltpu.CompilerParams(vmem_limit_bytes=VMEM_LIMIT),
        cost_estimate=pl.CostEstimate(flops=int(cost * 1.1e9), bytes_accessed=0, transcendentals=0),
        name=name,
    )(*args)


def swap_near(value, axis):
    return lax.ppermute(value, axis, [(i, i ^ 1) for i in range(lax.axis_size(axis))])


def swap_far(value, axis):
    count = lax.axis_size(axis)
    pairs = []
    for i in range(1, count, 2):
        pairs += [(i, (i + 1) % count), ((i + 1) % count, i)]
    return lax.ppermute(value, axis, pairs)


def from_other_half(value):
    return lax.ppermute(value, "tx", [(i, i ^ 3) for i in range(lax.axis_size("tx"))])


def on_device(source, guess, coefficient, leaf_map, body_map):
    dma = pltpu.SemaphoreType.DMA
    strip = ((SEG, 2, RHS), B16)
    *strips, own, sent = call(
        front_kernel, "front",
        [strip, strip, strip, ((2, 256, 256), F32), ((STRIP + 128, 128), WIRE)],
        guess, guess.reshape(SEG * SEG * 2, RHS), leaf_map[0, 0], kept=3,
        scratch=[pltpu.VMEM((2, 256, 256), F32), dma((5,))],
    )
    row_k, col_j, col_l = [strip.reshape(128, RHS) for strip in strips]
    partner = swap_near(sent, "tx")
    across_k = swap_far(row_k, "tx")
    across_l = swap_far(col_l, "ty")
    across_j = swap_near(col_j, "ty")
    flat, body = call(
        stencil_kernel, "stencil",
        [((SEG * SEG, 2 * RHS), F32), ((512, SEG * SEG), B16)],
        source.reshape(SEG * SEG * 2, RHS), guess.reshape(SEG * SEG * 2, RHS), coefficient,
        body_map.reshape(512, SEG * SEG), kept=4, cost=1.0,
        scratch=[
            pltpu.VMEM((SEG * SEG * 2, RHS), B16), pltpu.VMEM((SEG * SEG * 2, RHS), B16),
            pltpu.VMEM((SEG, SEG), F32), dma((BLOCKS,)), dma((BLOCKS,)), dma((BLOCKS,)), dma(()),
        ],
    )
    own_load, sent_load = call(
        leaf_kernel, "leaf_loads", [((2, 256, RHS), F32), ((2, 192, RHS), WIRE)],
        flat, body, across_j, across_k, across_l, partner, cost=2.5,
        scratch=[pltpu.VMEM((512, 2 * RHS), F32), pltpu.VMEM((128, RHS), F32), pltpu.VMEM((128, RHS), F32)],
    )
    partner, sent_load = lax.optimization_barrier((partner, sent_load))
    partner_load = swap_near(sent_load, "tx")

    face1, keep1, gain1 = call(
        merge_rows_kernel, "merge_rows",
        [((2, 128, 384), F32), ((2, 128, 384), F32), ((2, 256, 128), F32)], own, partner, cost=COSTS[4],
    )
    face1_across = swap_near(face1, "ty")
    load1, keep_load1 = call(
        load_rows_kernel, "load_rows", [((2, 128, RHS), F32)] * 2, own_load, partner_load, gain1, cost=COSTS[0]
    )
    load1_across = swap_near(load1, "ty")
    map2, near2, out_map2, gain2 = call(
        merge_cols_kernel, "merge_cols",
        [((2, 64, 512), F32), ((2, 64, 128), WIRE), ((2, 64, 512), F32), ((2, 128, 256), F32)],
        face1, face1_across, keep1, cost=COSTS[1],
    )
    far_near = from_other_half(near2)
    face2, rest2, out2 = call(
        load_cols_kernel, "load_cols", [((2, 64, 640), F32), ((2, 64, 512), WIRE), ((2, 64, 640), F32)],
        load1, load1_across, keep_load1, gain2, map2, out_map2, cost=COSTS[2],
    )
    face2_mate = swap_near(face2, "ty")
    far_rest = from_other_half(rest2)
    far_near_mate = swap_near(far_near, "ty")
    carried, mine = call(
        top_solve_kernel, "top_solve", [((2, 64, 128), F32), ((2, 64, 512), F32)],
        face2, face2_mate, far_near, far_near_mate, out2, cost=COSTS[3],
    )
    far_rest, carried = lax.optimization_barrier((far_rest, carried))
    far_rest_mate = swap_near(far_rest, "ty")
    top_map, top_out = call(
        top_kernel, "merge_top", [((2, 64, 768), F32), ((2, 64, RHS), F32)],
        carried, mine, far_rest, far_rest_mate,
    )
    return top_map[None, None], top_out[None, None]


def solution(mesh):
    placed = (
        P("tx", "ty", None, None),
        P("tx", "ty", None, None),
        P("tx", "ty"),
        P("tx", "ty", None, None, None),
        P("tx", "ty", None, None, None),
    )
    return jax.shard_map(
        on_device,
        mesh=mesh,
        in_specs=placed,
        out_specs=(P("tx", "ty", None, None, None), P("tx", "ty", None, None, None)),
        check_vma=False,
    )
```

```python
import jax
import jax.numpy as jnp
from jax import lax
from jax.experimental import pallas as pl
from jax.experimental.pallas import tpu as pltpu
from jax.sharding import PartitionSpec as P

F32 = jnp.float32
B16 = jnp.bfloat16
SQUARINGS = 8
SEG = 64
RHS = 128
WIRE = B16
VMEM_LIMIT = 24 * 1024 * 1024


def roles():
    row = lax.axis_index("tx")
    col = lax.axis_index("ty")
    even = (row & 1) == 0
    left = (col & 1) == 0
    inner = (((row + 1) >> 1) & 1) == 1
    upper = ((row >> 1) & 1) == 1
    return even, left, inner, upper


def side_order(even, left):
    return (
        jnp.where(even, 2, 0),
        jnp.where(left, 1, 3),
        jnp.where(even, 0, 2),
        jnp.where(left, 3, 1),
    )


def low_half(shape):
    return lax.broadcasted_iota(jnp.int32, shape, len(shape) - 1) % 128 < SEG


def half_roll(value):
    return jnp.concatenate([value[:, SEG:], value[:, :SEG]], axis=1)


def split(value):
    high = value.astype(B16)
    return high, (value - high.astype(F32)).astype(B16)


def times_i(stacked):
    half = stacked.shape[0] // 2
    return jnp.concatenate([-stacked[half:], stacked[:half]], axis=0)


def embed(stacked):
    return jnp.concatenate([stacked, times_i(stacked)], axis=1)


def dot(left, right):
    return jnp.dot(left, right, preferred_element_type=F32)


def dot_split(left, right):
    return dot(left[0], right[0]) + (dot(left[0], right[1]) + dot(left[1], right[0]))


def complex_dot(left, right):
    lefts = split(left)
    return dot_split((embed(lefts[0]), embed(lefts[1])), split(right))


def neumann_small(power):
    power = embed(power)
    rows = lax.broadcasted_iota(jnp.int32, power.shape, 0)
    cols = lax.broadcasted_iota(jnp.int32, power.shape, 1)
    total = power + jnp.where(rows == cols, 1.0, 0.0).astype(F32)
    parts = split(power)
    power = dot_split(parts, parts)
    for k in range(1, SQUARINGS):
        last = k + 1 == SQUARINGS
        both = total if last else jnp.concatenate([power, total], axis=1)
        if k < 2:
            step = dot_split(split(power), split(both))
        else:
            step = dot(power.astype(B16), both.astype(B16))
        if not last:
            power = step[:, :128]
            step = step[:, 128:]
        total = total + step
    return total


def neumann(power):
    size = power.shape[1]
    rows = lax.broadcasted_iota(jnp.int32, power.shape, 0)
    cols = lax.broadcasted_iota(jnp.int32, power.shape, 1)
    total = power + jnp.where(rows == cols, 1.0, 0.0).astype(F32)
    power = complex_dot(power, power)
    for k in range(1, SQUARINGS):
        both = total
        if k + 1 < SQUARINGS:
            both = jnp.concatenate([power, total], axis=1)
        if k < 2:
            step = complex_dot(power, both)
        else:
            step = dot(embed(power.astype(B16)), both.astype(B16))
        if k + 1 < SQUARINGS:
            power = step[:, :size]
            step = step[:, size:]
        total = total + step
    return total


def stack(ref, begin, length):
    return jnp.concatenate([ref[0, begin : begin + length], ref[1, begin : begin + length]], axis=0).astype(F32)


def store_stacked(ref, value, begin=0):
    half = value.shape[0] // 2
    ref[0, begin : begin + half] = value[:half].astype(ref.dtype)
    ref[1, begin : begin + half] = value[half:].astype(ref.dtype)


def rows_of(stacked, begin, length):
    half = stacked.shape[0] // 2
    return jnp.concatenate(
        [stacked[begin : begin + length], stacked[half + begin : half + begin + length]], axis=0
    )


def join_rows(parts):
    halves = [p.shape[0] // 2 for p in parts]
    return jnp.concatenate(
        [p[:h] for p, h in zip(parts, halves)] + [p[h:] for p, h in zip(parts, halves)], axis=0
    )


STRIP = 12 * SEG


def front_kernel(guess_ref, cells_ref, leaf_ref, row_k, col_j, col_l, own_ref, send_ref, leaf, sems):
    even, left, inner, _ = roles()
    row = jnp.where(even, SEG - 1, 0)
    col = jnp.where(left, SEG - 1, 0)
    copies = [
        pltpu.make_async_copy(
            cells_ref.at[pl.ds(pl.multiple_of(row * 128, 128), 128)], send_ref.at[pl.ds(STRIP, 128)], sems.at[0]
        ),
        pltpu.make_async_copy(guess_ref.at[SEG - 1 - row], row_k, sems.at[1]),
        pltpu.make_async_copy(guess_ref.at[:, col], col_j, sems.at[2]),
        pltpu.make_async_copy(guess_ref.at[:, SEG - 1 - col], col_l, sems.at[3]),
        pltpu.make_async_copy(leaf_ref, leaf, sems.at[4]),
    ]
    for copy in copies:
        copy.start()
    copies[4].wait()
    low = low_half((SEG, 128))
    crossed = (low & even) | (~low & ~left)
    for part in range(2):
        for place, side in enumerate(side_order(even, left)):
            rows = leaf[part, pl.ds(pl.multiple_of(side * SEG, SEG), SEG), :]
            first = rows[:, :128]
            second = rows[:, 128:]
            near = jnp.where(crossed, second, first)
            far = jnp.where(crossed, first, second)
            near = jnp.where(inner, half_roll(near), near)
            own_ref[part, place * SEG : (place + 1) * SEG, :128] = near
            own_ref[part, place * SEG : (place + 1) * SEG, 128:] = far
            if place < 3:
                at = (part * 3 + place) * 2 * SEG
                send_ref[at : at + SEG] = near.astype(send_ref.dtype)
                send_ref[at + SEG : at + 2 * SEG] = far.astype(send_ref.dtype)
    for copy in copies[:4]:
        copy.wait()


def planes_matrix(size=2 * SEG):
    row = lax.broadcasted_iota(jnp.int32, (size, size), 0)
    col = lax.broadcasted_iota(jnp.int32, (size, size), 1)
    return jnp.where(col == 2 * (row % SEG) + row // SEG, 1.0, 0.0).astype(B16)


def stencil_matrix():
    width = 2 * SEG
    row = lax.broadcasted_iota(jnp.int32, (width, width), 0)
    col = lax.broadcasted_iota(jnp.int32, (width, width), 1)
    apart = jnp.abs(col - 2 * (row % SEG) - row // SEG)
    own = jnp.where(apart == 0, 1.0, 0.0).astype(F32)
    beside = jnp.where(apart == 2, 1.0, 0.0).astype(F32)
    ahead = jnp.concatenate([own, beside - 4.0 * own], axis=1)
    value = jnp.concatenate([jnp.zeros_like(own), own], axis=1)
    return jnp.concatenate([ahead, value], axis=0).astype(B16)


COSTS = (5.0, 3.0, 0.4, 0.8, 3.0)
BLOCK = 16
BLOCKS = SEG // BLOCK


def stencil_kernel(source, guess, coef_rows, flat_ref, diagonal_ref):
    width = 2 * SEG
    chunk = BLOCK * width
    span = BLOCK * SEG
    table = stencil_matrix()
    planes = planes_matrix()
    diagonal_ref[...] = coef_rows[...]

    def block(i, carry):
        base = i * chunk

        def rows_at(ref, begin):
            return ref[pl.ds(pl.multiple_of(begin, width), width), :]

        below = rows_at(guess, jnp.maximum(base - width, 0))
        above = rows_at(guess, jnp.minimum(base + chunk, SEG * width - width))
        outer = dot(planes, jnp.concatenate([below, above], axis=1))
        values = {
            -1: jnp.where(i == 0, 0.0, outer[:, :RHS]),
            BLOCK: jnp.where(i == BLOCKS - 1, 0.0, outer[:, RHS:]),
        }
        ahead = {}
        coef = coef_rows[pl.ds(pl.multiple_of(i * BLOCK, BLOCK), BLOCK), :].T

        def finish(r):
            wave = jnp.broadcast_to(coef[:, r : r + 1], (SEG, RHS))
            sums = ahead[r] + (values[r - 1] + values[r + 1])
            real_part = values[r][:SEG]
            imag_part = values[r][SEG:]
            cells = pl.ds(pl.multiple_of(i * span + r * SEG, SEG), SEG)
            flat_ref[cells, :RHS] = sums[:SEG] + wave * (real_part - 0.5 * imag_part)
            flat_ref[cells, RHS:] = sums[SEG:] + wave * (imag_part + 0.5 * real_part)

        for k in range(0, BLOCK, 2):
            pair = [
                jnp.concatenate([rows_at(source, base + r * width), rows_at(guess, base + r * width)], axis=0)
                for r in (k, k + 1)
            ]
            both = dot(table, jnp.concatenate(pair, axis=1))
            for j, r in enumerate((k, k + 1)):
                ahead[r] = both[:width, j * RHS : (j + 1) * RHS]
                values[r] = both[width:, j * RHS : (j + 1) * RHS]
            if k > 0:
                finish(k - 1)
            finish(k)
        finish(BLOCK - 1)
        return carry

    lax.fori_loop(0, BLOCKS, block, 0)


def leaf_kernel(
    flat_ref, body_ref, across_j, across_k, across_l, partner_ref, own_ref, send_ref, total, west_ref, east_ref
):
    even, left, _, _ = roles()
    at_row = lax.axis_index("tx")
    at_col = lax.axis_index("ty")
    strips = dot(planes_matrix(), jnp.concatenate([partner_ref[STRIP:], across_k[...]], axis=1))
    south = jnp.where(even, strips[:, RHS:], strips[:, :RHS])
    north = jnp.where(even, strips[:, :RHS], strips[:, RHS:])
    south = jnp.where(at_row == 0, 0.0, south)
    north = jnp.where(at_row == lax.axis_size("tx") - 1, 0.0, north)
    near = across_j[...].astype(F32)
    far = across_l[...].astype(F32)
    west_ref[...] = jnp.where(at_col == 0, 0.0, jnp.where(left, far, near))
    east_ref[...] = jnp.where(at_col == lax.axis_size("ty") - 1, 0.0, jnp.where(left, near, far))
    row8 = lax.broadcasted_iota(jnp.int32, (8, RHS), 0)
    span = BLOCK * SEG

    def block(i):
        cells = []
        for r in range(BLOCK):
            parts = []
            for c in range(2):
                rows = pl.ds(pl.multiple_of(i * span + r * SEG, SEG), SEG)
                flat = flat_ref[rows, c * RHS : (c + 1) * RHS]
                if r == 0:
                    flat = flat + jnp.where(i == 0, south[c * SEG : (c + 1) * SEG], 0.0)
                if r == BLOCK - 1:
                    flat = flat + jnp.where(i == BLOCKS - 1, north[c * SEG : (c + 1) * SEG], 0.0)
                at = 2 * (i * BLOCK + r) + c
                begin = flat[:8] + jnp.where(row8 == 0, west_ref[pl.ds(at, 1), :], 0.0)
                end = flat[SEG - 8 :] + jnp.where(row8 == 7, east_ref[pl.ds(at, 1), :], 0.0)
                parts.append(jnp.concatenate([begin, flat[8 : SEG - 8], end], axis=0).astype(B16))
            cells.append(jnp.concatenate(parts, axis=1))
        return dot(body_ref[:, pl.ds(pl.multiple_of(i * span, span), span)], jnp.concatenate(cells, axis=0))

    total[...] = block(0)

    def add(i, carry):
        total[...] += block(i)
        return carry

    lax.fori_loop(1, BLOCKS, add, 0)
    half = total.shape[0] // 2
    real_part = total[:half, :RHS] - total[half:, RHS:]
    imag_part = total[:half, RHS:] + total[half:, :RHS]
    total[:half, :RHS] = real_part
    total[half:, :RHS] = imag_part
    for part in range(2):
        for place, side in enumerate(side_order(even, left)):
            rows = total[pl.ds(pl.multiple_of(part * half + side * SEG, SEG), SEG), :RHS]
            own_ref[part, place * SEG : (place + 1) * SEG] = rows
            if place < 3:
                send_ref[part, place * SEG : (place + 1) * SEG] = rows.astype(send_ref.dtype)


def merge_rows_kernel(own_ref, partner_ref, face_ref, keep_ref, gain_ref):
    _, _, inner, _ = roles()

    def sent(place, part):
        at = (part * 3 + place) * 2 * SEG
        return jnp.concatenate([partner_ref[at : at + SEG], partner_ref[at + SEG : at + 2 * SEG]], axis=1)

    def pick(place):
        mine = stack(own_ref, place * SEG, SEG)
        theirs = jnp.concatenate([sent(place, 0), sent(place, 1)], axis=0).astype(F32)
        return jnp.where(inner, mine, theirs), jnp.where(inner, theirs, mine)

    n_i, u_i = pick(0)
    n_j, u_j = pick(1)
    n_k, _ = pick(2)
    out = jnp.where(inner, stack(own_ref, 3 * SEG, SEG), stack(own_ref, 2 * SEG, SEG))
    inner_n = n_i[:, SEG:128]
    inner_u = u_i[:, :SEG]
    solved = neumann_small(complex_dot(inner_u, inner_n))
    carried = dot_split(split(solved), split(inner_u))
    into_n = jnp.concatenate([carried, -solved[:, :SEG]], axis=1)
    rows = lax.broadcasted_iota(jnp.int32, (128, 128), 0)
    cols = lax.broadcasted_iota(jnp.int32, (128, 128), 1)
    unit = jnp.where((rows == cols) & (cols < SEG), 1.0, 0.0).astype(F32)
    into_u = -unit - complex_dot(inner_n, into_n)
    gain_n = complex_dot(join_rows([n_j[:, SEG:128], n_k[:, SEG:128]]), into_n)
    gain_u = complex_dot(u_j[:, :SEG], into_u)
    gain_out = complex_dot(
        jnp.where(inner, out[:, SEG:128], out[:, :SEG]), jnp.where(inner, into_n, into_u)
    )
    gain = join_rows([rows_of(gain_n, 0, SEG), gain_u, rows_of(gain_n, SEG, SEG), gain_out])
    store_stacked(gain_ref, gain)
    zero = jnp.zeros_like(n_j)
    in_n = complex_dot(gain[:, :SEG], n_i) + join_rows([n_j, zero, n_k, jnp.where(inner, out, 0.0)])
    in_u = complex_dot(gain[:, SEG:], u_i) + join_rows([zero, u_j, zero, jnp.where(inner, 0.0, out)])
    joint = jnp.where(low_half((512, 128)), in_n[:, :128], in_u[:, :128])
    merged = jnp.concatenate([joint, in_n[:, 128:], in_u[:, 128:]], axis=1)
    store_stacked(face_ref, rows_of(merged, 0, 128))
    store_stacked(keep_ref, rows_of(merged, 128, 128))


def load_rows_kernel(own_ref, partner_ref, gain_ref, face_ref, keep_ref):
    _, _, inner, _ = roles()

    def pick(place):
        mine = stack(own_ref, place * SEG, SEG)
        theirs = stack(partner_ref, place * SEG, SEG)
        return jnp.where(inner, mine, theirs), jnp.where(inner, theirs, mine)

    n_i, u_i = pick(0)
    n_j, u_j = pick(1)
    n_k, _ = pick(2)
    out = jnp.where(inner, stack(own_ref, 3 * SEG, SEG), stack(own_ref, 2 * SEG, SEG))
    merged = complex_dot(stack(gain_ref, 0, 256), join_rows([n_i, u_i])) + join_rows([n_j, u_j, n_k, out])
    store_stacked(face_ref, rows_of(merged, 0, 128))
    store_stacked(keep_ref, rows_of(merged, 128, 128))


def merge_cols_kernel(own_ref, across_ref, keep_ref, face_ref, send_near, out_ref, gain_ref):
    _, left, _, upper = roles()
    own = stack(own_ref, 0, 128)
    across = stack(across_ref, 0, 128)
    keep = stack(keep_ref, 0, 128)
    inverse = neumann(complex_dot(across[:, :128], own[:, :128]))
    bounced = complex_dot(across[:, :128], own[:, 128:])
    carried = complex_dot(keep[:, :128], inverse)
    gained = complex_dot(carried, jnp.concatenate([bounced, across], axis=1))
    store_stacked(gain_ref, jnp.concatenate([gained[:, 256:384], -carried], axis=1))
    mine = keep[:, 128:] + gained[:, :256]
    theirs = -gained[:, 384:]
    west = jnp.where(left, mine, theirs)
    east = jnp.where(left, theirs, mine)
    low = low_half((256, 128))
    west_n, west_u = west[:, :128], west[:, 128:]
    east_n, east_u = east[:, :128], east[:, 128:]
    roll_wn, roll_wu, roll_en, roll_eu = [half_roll(v) for v in (west_n, west_u, east_n, east_u)]
    inner_k = jnp.where(low, west_n, roll_en)
    outer_k = jnp.where(low, west_u, roll_eu)
    east_l = jnp.where(upper, jnp.where(low, roll_en, east_u), jnp.where(low, roll_eu, east_n))
    west_l = jnp.where(upper, jnp.where(low, roll_wn, west_u), jnp.where(low, roll_wu, west_n))
    merged = jnp.concatenate([inner_k, outer_k, east_l, west_l], axis=1)
    face = rows_of(merged, 0, SEG)
    store_stacked(face_ref, face)
    store_stacked(send_near, face[:, :128])
    store_stacked(out_ref, rows_of(merged, SEG, SEG))


def load_cols_kernel(own_ref, across_ref, keep_ref, gain_ref, map_ref, out_map, face_ref, send_ref, out_ref):
    sides = join_rows([stack(own_ref, 0, 128), stack(across_ref, 0, 128)])
    merged = stack(keep_ref, 0, 128) + complex_dot(stack(gain_ref, 0, 128), sides)
    for half in range(2):
        face_ref[half, :, :512] = map_ref[half]
        face_ref[half, :, 512:] = merged[half * 128 : half * 128 + SEG]
        send_ref[half, :, :384] = map_ref[half, :, 128:].astype(send_ref.dtype)
        send_ref[half, :, 384:] = merged[half * 128 : half * 128 + SEG].astype(send_ref.dtype)
        out_ref[half, :, :512] = out_map[half]
        out_ref[half, :, 512:] = merged[half * 128 + SEG : half * 128 + 128]


def sides_of(mine_ref, theirs_ref):
    _, left, _, _ = roles()
    mine = stack(mine_ref, 0, SEG)
    theirs = stack(theirs_ref, 0, SEG)
    return join_rows([jnp.where(left, mine, theirs), jnp.where(left, theirs, mine)])


def top_solve_kernel(own_ref, mate_ref, far_ref, far_mate_ref, out_ref, carried_ref, mine_ref):
    near = sides_of(own_ref, mate_ref)
    far = sides_of(far_ref, far_mate_ref)
    rows = stack(out_ref, 0, SEG)
    exact = embed(far.astype(WIRE))
    reflected = dot(exact, split(near)[0]) + dot(exact, split(near)[1])
    inverse = neumann(reflected[:, :128])
    bounced = reflected[:, 128:]
    carried = complex_dot(rows[:, :128], inverse)
    store_stacked(carried_ref, carried)
    store_stacked(mine_ref, rows[:, 128:] + complex_dot(carried, bounced))


def top_kernel(carried_ref, mine_ref, far_ref, far_mate_ref, map_ref, load_ref):
    _, _, _, upper = roles()
    far = sides_of(far_ref, far_mate_ref).astype(B16)
    mine = stack(mine_ref, 0, SEG)
    lefts = split(stack(carried_ref, 0, SEG))
    theirs = -(dot(embed(lefts[0]), far) + dot(embed(lefts[1]), far))
    store_stacked(load_ref, mine[:, 384:] + theirs[:, 384:])
    lower_part = jnp.where(upper, theirs[:, :384], mine[:, :384])
    upper_part = jnp.where(upper, mine[:, :384], theirs[:, :384])
    store_stacked(
        map_ref,
        jnp.concatenate(
            [lower_part, upper_part[:, 128:256], upper_part[:, :128], upper_part[:, 256:]], axis=1
        ),
    )


def call(kernel, name, outs, *args, kept=0, scratch=(), cost=1.0):
    args = [pltpu.with_memory_space_constraint(v, pltpu.HBM) if i < kept else v for i, v in enumerate(args)]
    return pl.pallas_call(
        kernel,
        in_specs=[pl.BlockSpec(memory_space=pltpu.HBM if i < kept else pltpu.VMEM) for i in range(len(args))],
        out_shape=[jax.ShapeDtypeStruct(shape, dtype) for shape, dtype in outs],
        scratch_shapes=list(scratch),
        compiler_params=pltpu.CompilerParams(vmem_limit_bytes=VMEM_LIMIT),
        cost_estimate=pl.CostEstimate(flops=int(cost * 1.1e9), bytes_accessed=0, transcendentals=0),
        name=name,
    )(*args)


def swap_near(value, axis):
    return lax.ppermute(value, axis, [(i, i ^ 1) for i in range(lax.axis_size(axis))])


def swap_far(value, axis):
    count = lax.axis_size(axis)
    pairs = []
    for i in range(1, count, 2):
        pairs += [(i, (i + 1) % count), ((i + 1) % count, i)]
    return lax.ppermute(value, axis, pairs)


def from_other_half(value):
    return lax.ppermute(value, "tx", [(i, i ^ 3) for i in range(lax.axis_size("tx"))])


def on_device(source, guess, coefficient, leaf_map, body_map):
    dma = pltpu.SemaphoreType.DMA
    strip = ((SEG, 2, RHS), B16)
    *strips, own, sent = call(
        front_kernel, "front",
        [strip, strip, strip, ((2, 256, 256), F32), ((STRIP + 128, 128), WIRE)],
        guess, guess.reshape(SEG * SEG * 2, RHS), leaf_map[0, 0], kept=3,
        scratch=[pltpu.VMEM((2, 256, 256), F32), dma((5,))],
    )
    row_k, col_j, col_l = [strip.reshape(128, RHS) for strip in strips]
    partner = swap_near(sent, "tx")
    across_k = swap_far(row_k, "tx")
    across_l = swap_far(col_l, "ty")
    across_j = swap_near(col_j, "ty")
    flat, _ = call(
        stencil_kernel, "stencil", [((SEG * SEG, 2 * RHS), F32), ((SEG, SEG), F32)],
        source.reshape(SEG * SEG * 2, RHS), guess.reshape(SEG * SEG * 2, RHS), coefficient, cost=1.0,
    )
    body = body_map.reshape(512, SEG * SEG)
    own_load, sent_load = call(
        leaf_kernel, "leaf_loads", [((2, 256, RHS), F32), ((2, 192, RHS), WIRE)],
        flat, body, across_j, across_k, across_l, partner, cost=2.5,
        scratch=[pltpu.VMEM((512, 2 * RHS), F32), pltpu.VMEM((128, RHS), F32), pltpu.VMEM((128, RHS), F32)],
    )
    partner, sent_load = lax.optimization_barrier((partner, sent_load))
    partner_load = swap_near(sent_load, "tx")

    face1, keep1, gain1 = call(
        merge_rows_kernel, "merge_rows",
        [((2, 128, 384), F32), ((2, 128, 384), F32), ((2, 256, 128), F32)], own, partner, cost=COSTS[4],
    )
    face1_across = swap_near(face1, "ty")
    load1, keep_load1 = call(
        load_rows_kernel, "load_rows", [((2, 128, RHS), F32)] * 2, own_load, partner_load, gain1, cost=COSTS[0]
    )
    load1_across = swap_near(load1, "ty")
    map2, near2, out_map2, gain2 = call(
        merge_cols_kernel, "merge_cols",
        [((2, 64, 512), F32), ((2, 64, 128), WIRE), ((2, 64, 512), F32), ((2, 128, 256), F32)],
        face1, face1_across, keep1, cost=COSTS[1],
    )
    far_near = from_other_half(near2)
    face2, rest2, out2 = call(
        load_cols_kernel, "load_cols", [((2, 64, 640), F32), ((2, 64, 512), WIRE), ((2, 64, 640), F32)],
        load1, load1_across, keep_load1, gain2, map2, out_map2, cost=COSTS[2],
    )
    face2_mate = swap_near(face2, "ty")
    far_rest = from_other_half(rest2)
    far_near_mate = swap_near(far_near, "ty")
    carried, mine = call(
        top_solve_kernel, "top_solve", [((2, 64, 128), F32), ((2, 64, 512), F32)],
        face2, face2_mate, far_near, far_near_mate, out2, cost=COSTS[3],
    )
    far_rest, carried = lax.optimization_barrier((far_rest, carried))
    far_rest_mate = swap_near(far_rest, "ty")
    top_map, top_out = call(
        top_kernel, "merge_top", [((2, 64, 768), F32), ((2, 64, RHS), F32)],
        carried, mine, far_rest, far_rest_mate,
    )
    return top_map[None, None], top_out[None, None]


def solution(mesh):
    placed = (
        P("tx", "ty", None, None),
        P("tx", "ty", None, None),
        P("tx", "ty"),
        P("tx", "ty", None, None, None),
        P("tx", "ty", None, None, None),
    )
    return jax.shard_map(
        on_device,
        mesh=mesh,
        in_specs=placed,
        out_specs=(P("tx", "ty", None, None, None), P("tx", "ty", None, None, None)),
        check_vma=False,
    )
```

```python
import jax
import jax.numpy as jnp
from jax import lax
from jax.experimental import pallas as pl
from jax.experimental.pallas import tpu as pltpu
from jax.sharding import PartitionSpec as P

F32 = jnp.float32
B16 = jnp.bfloat16
SQUARINGS = 8
SEG = 64
RHS = 128
WIRE = B16
VMEM_LIMIT = 24 * 1024 * 1024


def roles():
    row = lax.axis_index("tx")
    col = lax.axis_index("ty")
    even = (row & 1) == 0
    left = (col & 1) == 0
    inner = (((row + 1) >> 1) & 1) == 1
    upper = ((row >> 1) & 1) == 1
    return even, left, inner, upper


def side_order(even, left):
    return (
        jnp.where(even, 2, 0),
        jnp.where(left, 1, 3),
        jnp.where(even, 0, 2),
        jnp.where(left, 3, 1),
    )


def low_half(shape):
    return lax.broadcasted_iota(jnp.int32, shape, len(shape) - 1) % 128 < SEG


def half_roll(value):
    return jnp.concatenate([value[:, SEG:], value[:, :SEG]], axis=1)


def split(value):
    high = value.astype(B16)
    return high, (value - high.astype(F32)).astype(B16)


def times_i(stacked):
    half = stacked.shape[0] // 2
    return jnp.concatenate([-stacked[half:], stacked[:half]], axis=0)


def embed(stacked):
    return jnp.concatenate([stacked, times_i(stacked)], axis=1)


def dot(left, right):
    return jnp.dot(left, right, preferred_element_type=F32)


def dot_split(left, right):
    return dot(left[0], right[0]) + (dot(left[0], right[1]) + dot(left[1], right[0]))


def complex_dot(left, right):
    lefts = split(left)
    return dot_split((embed(lefts[0]), embed(lefts[1])), split(right))


def neumann_small(power):
    power = embed(power)
    rows = lax.broadcasted_iota(jnp.int32, power.shape, 0)
    cols = lax.broadcasted_iota(jnp.int32, power.shape, 1)
    total = power + jnp.where(rows == cols, 1.0, 0.0).astype(F32)
    parts = split(power)
    power = dot_split(parts, parts)
    for k in range(1, SQUARINGS):
        last = k + 1 == SQUARINGS
        both = total if last else jnp.concatenate([power, total], axis=1)
        if k < 1:
            step = dot_split(split(power), split(both))
        else:
            step = dot(power.astype(B16), both.astype(B16))
        if not last:
            power = step[:, :128]
            step = step[:, 128:]
        total = total + step
    return total


def neumann(power):
    size = power.shape[1]
    rows = lax.broadcasted_iota(jnp.int32, power.shape, 0)
    cols = lax.broadcasted_iota(jnp.int32, power.shape, 1)
    total = power + jnp.where(rows == cols, 1.0, 0.0).astype(F32)
    power = complex_dot(power, power)
    for k in range(1, SQUARINGS):
        both = total
        if k + 1 < SQUARINGS:
            both = jnp.concatenate([power, total], axis=1)
        if k < 1:
            step = complex_dot(power, both)
        else:
            step = dot(embed(power.astype(B16)), both.astype(B16))
        if k + 1 < SQUARINGS:
            power = step[:, :size]
            step = step[:, size:]
        total = total + step
    return total


def stack(ref, begin, length):
    return jnp.concatenate([ref[0, begin : begin + length], ref[1, begin : begin + length]], axis=0).astype(F32)


def store_stacked(ref, value, begin=0):
    half = value.shape[0] // 2
    ref[0, begin : begin + half] = value[:half].astype(ref.dtype)
    ref[1, begin : begin + half] = value[half:].astype(ref.dtype)


def rows_of(stacked, begin, length):
    half = stacked.shape[0] // 2
    return jnp.concatenate(
        [stacked[begin : begin + length], stacked[half + begin : half + begin + length]], axis=0
    )


def join_rows(parts):
    halves = [p.shape[0] // 2 for p in parts]
    return jnp.concatenate(
        [p[:h] for p, h in zip(parts, halves)] + [p[h:] for p, h in zip(parts, halves)], axis=0
    )


STRIP = 12 * SEG


def front_kernel(guess_ref, cells_ref, leaf_ref, row_k, col_j, col_l, own_ref, send_ref, leaf, sems):
    even, left, inner, _ = roles()
    row = jnp.where(even, SEG - 1, 0)
    col = jnp.where(left, SEG - 1, 0)
    copies = [
        pltpu.make_async_copy(
            cells_ref.at[pl.ds(pl.multiple_of(row * 128, 128), 128)], send_ref.at[pl.ds(STRIP, 128)], sems.at[0]
        ),
        pltpu.make_async_copy(guess_ref.at[SEG - 1 - row], row_k, sems.at[1]),
        pltpu.make_async_copy(guess_ref.at[:, col], col_j, sems.at[2]),
        pltpu.make_async_copy(guess_ref.at[:, SEG - 1 - col], col_l, sems.at[3]),
        pltpu.make_async_copy(leaf_ref, leaf, sems.at[4]),
    ]
    for copy in copies:
        copy.start()
    copies[4].wait()
    low = low_half((SEG, 128))
    crossed = (low & even) | (~low & ~left)
    for part in range(2):
        for place, side in enumerate(side_order(even, left)):
            rows = leaf[part, pl.ds(pl.multiple_of(side * SEG, SEG), SEG), :]
            first = rows[:, :128]
            second = rows[:, 128:]
            near = jnp.where(crossed, second, first)
            far = jnp.where(crossed, first, second)
            near = jnp.where(inner, half_roll(near), near)
            own_ref[part, place * SEG : (place + 1) * SEG, :128] = near
            own_ref[part, place * SEG : (place + 1) * SEG, 128:] = far
            if place < 3:
                at = (part * 3 + place) * 2 * SEG
                send_ref[at : at + SEG] = near.astype(send_ref.dtype)
                send_ref[at + SEG : at + 2 * SEG] = far.astype(send_ref.dtype)
    for copy in copies[:4]:
        copy.wait()


def planes_matrix(size=2 * SEG):
    row = lax.broadcasted_iota(jnp.int32, (size, size), 0)
    col = lax.broadcasted_iota(jnp.int32, (size, size), 1)
    return jnp.where(col == 2 * (row % SEG) + row // SEG, 1.0, 0.0).astype(B16)


def stencil_matrix():
    width = 2 * SEG
    row = lax.broadcasted_iota(jnp.int32, (width, width), 0)
    col = lax.broadcasted_iota(jnp.int32, (width, width), 1)
    apart = jnp.abs(col - 2 * (row % SEG) - row // SEG)
    own = jnp.where(apart == 0, 1.0, 0.0).astype(F32)
    beside = jnp.where(apart == 2, 1.0, 0.0).astype(F32)
    ahead = jnp.concatenate([own, beside - 4.0 * own], axis=1)
    value = jnp.concatenate([jnp.zeros_like(own), own], axis=1)
    return jnp.concatenate([ahead, value], axis=0).astype(B16)


COSTS = (5.0, 3.0, 0.4, 0.8, 3.0)
BLOCK = 16
BLOCKS = SEG // BLOCK


def stencil_kernel(source, guess, coef_rows, flat_ref, diagonal_ref):
    width = 2 * SEG
    chunk = BLOCK * width
    span = BLOCK * SEG
    table = stencil_matrix()
    planes = planes_matrix()
    diagonal_ref[...] = coef_rows[...]

    def block(i, carry):
        base = i * chunk

        def rows_at(ref, begin):
            return ref[pl.ds(pl.multiple_of(begin, width), width), :]

        below = rows_at(guess, jnp.maximum(base - width, 0))
        above = rows_at(guess, jnp.minimum(base + chunk, SEG * width - width))
        outer = dot(planes, jnp.concatenate([below, above], axis=1))
        values = {
            -1: jnp.where(i == 0, 0.0, outer[:, :RHS]),
            BLOCK: jnp.where(i == BLOCKS - 1, 0.0, outer[:, RHS:]),
        }
        ahead = {}
        coef = coef_rows[pl.ds(pl.multiple_of(i * BLOCK, BLOCK), BLOCK), :].T

        def finish(r):
            wave = jnp.broadcast_to(coef[:, r : r + 1], (SEG, RHS))
            sums = ahead[r] + (values[r - 1] + values[r + 1])
            real_part = values[r][:SEG]
            imag_part = values[r][SEG:]
            cells = pl.ds(pl.multiple_of(i * span + r * SEG, SEG), SEG)
            flat_ref[cells, :RHS] = sums[:SEG] + wave * (real_part - 0.5 * imag_part)
            flat_ref[cells, RHS:] = sums[SEG:] + wave * (imag_part + 0.5 * real_part)

        for k in range(0, BLOCK, 2):
            pair = [
                jnp.concatenate([rows_at(source, base + r * width), rows_at(guess, base + r * width)], axis=0)
                for r in (k, k + 1)
            ]
            both = dot(table, jnp.concatenate(pair, axis=1))
            for j, r in enumerate((k, k + 1)):
                ahead[r] = both[:width, j * RHS : (j + 1) * RHS]
                values[r] = both[width:, j * RHS : (j + 1) * RHS]
            if k > 0:
                finish(k - 1)
            finish(k)
        finish(BLOCK - 1)
        return carry

    lax.fori_loop(0, BLOCKS, block, 0)


def leaf_kernel(
    flat_ref, body_ref, across_j, across_k, across_l, partner_ref, own_ref, send_ref, total, west_ref, east_ref
):
    even, left, _, _ = roles()
    at_row = lax.axis_index("tx")
    at_col = lax.axis_index("ty")
    strips = dot(planes_matrix(), jnp.concatenate([partner_ref[STRIP:], across_k[...]], axis=1))
    south = jnp.where(even, strips[:, RHS:], strips[:, :RHS])
    north = jnp.where(even, strips[:, :RHS], strips[:, RHS:])
    south = jnp.where(at_row == 0, 0.0, south)
    north = jnp.where(at_row == lax.axis_size("tx") - 1, 0.0, north)
    near = across_j[...].astype(F32)
    far = across_l[...].astype(F32)
    west_ref[...] = jnp.where(at_col == 0, 0.0, jnp.where(left, far, near))
    east_ref[...] = jnp.where(at_col == lax.axis_size("ty") - 1, 0.0, jnp.where(left, near, far))
    row8 = lax.broadcasted_iota(jnp.int32, (8, RHS), 0)
    span = BLOCK * SEG

    def block(i):
        cells = []
        for r in range(BLOCK):
            parts = []
            for c in range(2):
                rows = pl.ds(pl.multiple_of(i * span + r * SEG, SEG), SEG)
                flat = flat_ref[rows, c * RHS : (c + 1) * RHS]
                if r == 0:
                    flat = flat + jnp.where(i == 0, south[c * SEG : (c + 1) * SEG], 0.0)
                if r == BLOCK - 1:
                    flat = flat + jnp.where(i == BLOCKS - 1, north[c * SEG : (c + 1) * SEG], 0.0)
                at = 2 * (i * BLOCK + r) + c
                begin = flat[:8] + jnp.where(row8 == 0, west_ref[pl.ds(at, 1), :], 0.0)
                end = flat[SEG - 8 :] + jnp.where(row8 == 7, east_ref[pl.ds(at, 1), :], 0.0)
                parts.append(jnp.concatenate([begin, flat[8 : SEG - 8], end], axis=0).astype(B16))
            cells.append(jnp.concatenate(parts, axis=1))
        return dot(body_ref[:, pl.ds(pl.multiple_of(i * span, span), span)], jnp.concatenate(cells, axis=0))

    total[...] = block(0)

    def add(i, carry):
        total[...] += block(i)
        return carry

    lax.fori_loop(1, BLOCKS, add, 0)
    half = total.shape[0] // 2
    real_part = total[:half, :RHS] - total[half:, RHS:]
    imag_part = total[:half, RHS:] + total[half:, :RHS]
    total[:half, :RHS] = real_part
    total[half:, :RHS] = imag_part
    for part in range(2):
        for place, side in enumerate(side_order(even, left)):
            rows = total[pl.ds(pl.multiple_of(part * half + side * SEG, SEG), SEG), :RHS]
            own_ref[part, place * SEG : (place + 1) * SEG] = rows
            if place < 3:
                send_ref[part, place * SEG : (place + 1) * SEG] = rows.astype(send_ref.dtype)


def merge_rows_kernel(own_ref, partner_ref, face_ref, keep_ref, gain_ref):
    _, _, inner, _ = roles()

    def sent(place, part):
        at = (part * 3 + place) * 2 * SEG
        return jnp.concatenate([partner_ref[at : at + SEG], partner_ref[at + SEG : at + 2 * SEG]], axis=1)

    def pick(place):
        mine = stack(own_ref, place * SEG, SEG)
        theirs = jnp.concatenate([sent(place, 0), sent(place, 1)], axis=0).astype(F32)
        return jnp.where(inner, mine, theirs), jnp.where(inner, theirs, mine)

    n_i, u_i = pick(0)
    n_j, u_j = pick(1)
    n_k, _ = pick(2)
    out = jnp.where(inner, stack(own_ref, 3 * SEG, SEG), stack(own_ref, 2 * SEG, SEG))
    inner_n = n_i[:, SEG:128]
    inner_u = u_i[:, :SEG]
    solved = neumann_small(complex_dot(inner_u, inner_n))
    carried = dot_split(split(solved), split(inner_u))
    into_n = jnp.concatenate([carried, -solved[:, :SEG]], axis=1)
    rows = lax.broadcasted_iota(jnp.int32, (128, 128), 0)
    cols = lax.broadcasted_iota(jnp.int32, (128, 128), 1)
    unit = jnp.where((rows == cols) & (cols < SEG), 1.0, 0.0).astype(F32)
    into_u = -unit - complex_dot(inner_n, into_n)
    gain_n = complex_dot(join_rows([n_j[:, SEG:128], n_k[:, SEG:128]]), into_n)
    gain_u = complex_dot(u_j[:, :SEG], into_u)
    gain_out = complex_dot(
        jnp.where(inner, out[:, SEG:128], out[:, :SEG]), jnp.where(inner, into_n, into_u)
    )
    gain = join_rows([rows_of(gain_n, 0, SEG), gain_u, rows_of(gain_n, SEG, SEG), gain_out])
    store_stacked(gain_ref, gain)
    zero = jnp.zeros_like(n_j)
    in_n = complex_dot(gain[:, :SEG], n_i) + join_rows([n_j, zero, n_k, jnp.where(inner, out, 0.0)])
    in_u = complex_dot(gain[:, SEG:], u_i) + join_rows([zero, u_j, zero, jnp.where(inner, 0.0, out)])
    joint = jnp.where(low_half((512, 128)), in_n[:, :128], in_u[:, :128])
    merged = jnp.concatenate([joint, in_n[:, 128:], in_u[:, 128:]], axis=1)
    store_stacked(face_ref, rows_of(merged, 0, 128))
    store_stacked(keep_ref, rows_of(merged, 128, 128))


def load_rows_kernel(own_ref, partner_ref, gain_ref, face_ref, keep_ref):
    _, _, inner, _ = roles()

    def pick(place):
        mine = stack(own_ref, place * SEG, SEG)
        theirs = stack(partner_ref, place * SEG, SEG)
        return jnp.where(inner, mine, theirs), jnp.where(inner, theirs, mine)

    n_i, u_i = pick(0)
    n_j, u_j = pick(1)
    n_k, _ = pick(2)
    out = jnp.where(inner, stack(own_ref, 3 * SEG, SEG), stack(own_ref, 2 * SEG, SEG))
    merged = complex_dot(stack(gain_ref, 0, 256), join_rows([n_i, u_i])) + join_rows([n_j, u_j, n_k, out])
    store_stacked(face_ref, rows_of(merged, 0, 128))
    store_stacked(keep_ref, rows_of(merged, 128, 128))


def merge_cols_kernel(own_ref, across_ref, keep_ref, face_ref, send_near, out_ref, gain_ref):
    _, left, _, upper = roles()
    own = stack(own_ref, 0, 128)
    across = stack(across_ref, 0, 128)
    keep = stack(keep_ref, 0, 128)
    inverse = neumann(complex_dot(across[:, :128], own[:, :128]))
    bounced = complex_dot(across[:, :128], own[:, 128:])
    carried = complex_dot(keep[:, :128], inverse)
    gained = complex_dot(carried, jnp.concatenate([bounced, across], axis=1))
    store_stacked(gain_ref, jnp.concatenate([gained[:, 256:384], -carried], axis=1))
    mine = keep[:, 128:] + gained[:, :256]
    theirs = -gained[:, 384:]
    west = jnp.where(left, mine, theirs)
    east = jnp.where(left, theirs, mine)
    low = low_half((256, 128))
    west_n, west_u = west[:, :128], west[:, 128:]
    east_n, east_u = east[:, :128], east[:, 128:]
    roll_wn, roll_wu, roll_en, roll_eu = [half_roll(v) for v in (west_n, west_u, east_n, east_u)]
    inner_k = jnp.where(low, west_n, roll_en)
    outer_k = jnp.where(low, west_u, roll_eu)
    east_l = jnp.where(upper, jnp.where(low, roll_en, east_u), jnp.where(low, roll_eu, east_n))
    west_l = jnp.where(upper, jnp.where(low, roll_wn, west_u), jnp.where(low, roll_wu, west_n))
    merged = jnp.concatenate([inner_k, outer_k, east_l, west_l], axis=1)
    face = rows_of(merged, 0, SEG)
    store_stacked(face_ref, face)
    store_stacked(send_near, face[:, :128])
    store_stacked(out_ref, rows_of(merged, SEG, SEG))


def load_cols_kernel(own_ref, across_ref, keep_ref, gain_ref, map_ref, out_map, face_ref, send_ref, out_ref):
    sides = join_rows([stack(own_ref, 0, 128), stack(across_ref, 0, 128)])
    merged = stack(keep_ref, 0, 128) + complex_dot(stack(gain_ref, 0, 128), sides)
    for half in range(2):
        face_ref[half, :, :512] = map_ref[half]
        face_ref[half, :, 512:] = merged[half * 128 : half * 128 + SEG]
        send_ref[half, :, :384] = map_ref[half, :, 128:].astype(send_ref.dtype)
        send_ref[half, :, 384:] = merged[half * 128 : half * 128 + SEG].astype(send_ref.dtype)
        out_ref[half, :, :512] = out_map[half]
        out_ref[half, :, 512:] = merged[half * 128 + SEG : half * 128 + 128]


def sides_of(mine_ref, theirs_ref):
    _, left, _, _ = roles()
    mine = stack(mine_ref, 0, SEG)
    theirs = stack(theirs_ref, 0, SEG)
    return join_rows([jnp.where(left, mine, theirs), jnp.where(left, theirs, mine)])


def top_solve_kernel(own_ref, mate_ref, far_ref, far_mate_ref, out_ref, carried_ref, mine_ref):
    near = sides_of(own_ref, mate_ref)
    far = sides_of(far_ref, far_mate_ref)
    rows = stack(out_ref, 0, SEG)
    exact = embed(far.astype(WIRE))
    reflected = dot(exact, split(near)[0]) + dot(exact, split(near)[1])
    inverse = neumann(reflected[:, :128])
    bounced = reflected[:, 128:]
    carried = complex_dot(rows[:, :128], inverse)
    store_stacked(carried_ref, carried)
    store_stacked(mine_ref, rows[:, 128:] + complex_dot(carried, bounced))


def top_kernel(carried_ref, mine_ref, far_ref, far_mate_ref, map_ref, load_ref):
    _, _, _, upper = roles()
    far = sides_of(far_ref, far_mate_ref).astype(B16)
    mine = stack(mine_ref, 0, SEG)
    lefts = split(stack(carried_ref, 0, SEG))
    theirs = -(dot(embed(lefts[0]), far) + dot(embed(lefts[1]), far))
    store_stacked(load_ref, mine[:, 384:] + theirs[:, 384:])
    lower_part = jnp.where(upper, theirs[:, :384], mine[:, :384])
    upper_part = jnp.where(upper, mine[:, :384], theirs[:, :384])
    store_stacked(
        map_ref,
        jnp.concatenate(
            [lower_part, upper_part[:, 128:256], upper_part[:, :128], upper_part[:, 256:]], axis=1
        ),
    )


def call(kernel, name, outs, *args, kept=0, scratch=(), cost=1.0):
    args = [pltpu.with_memory_space_constraint(v, pltpu.HBM) if i < kept else v for i, v in enumerate(args)]
    return pl.pallas_call(
        kernel,
        in_specs=[pl.BlockSpec(memory_space=pltpu.HBM if i < kept else pltpu.VMEM) for i in range(len(args))],
        out_shape=[jax.ShapeDtypeStruct(shape, dtype) for shape, dtype in outs],
        scratch_shapes=list(scratch),
        compiler_params=pltpu.CompilerParams(vmem_limit_bytes=VMEM_LIMIT),
        cost_estimate=pl.CostEstimate(flops=int(cost * 1.1e9), bytes_accessed=0, transcendentals=0),
        name=name,
    )(*args)


def swap_near(value, axis):
    return lax.ppermute(value, axis, [(i, i ^ 1) for i in range(lax.axis_size(axis))])


def swap_far(value, axis):
    count = lax.axis_size(axis)
    pairs = []
    for i in range(1, count, 2):
        pairs += [(i, (i + 1) % count), ((i + 1) % count, i)]
    return lax.ppermute(value, axis, pairs)


def from_other_half(value):
    return lax.ppermute(value, "tx", [(i, i ^ 3) for i in range(lax.axis_size("tx"))])


def on_device(source, guess, coefficient, leaf_map, body_map):
    dma = pltpu.SemaphoreType.DMA
    strip = ((SEG, 2, RHS), B16)
    *strips, own, sent = call(
        front_kernel, "front",
        [strip, strip, strip, ((2, 256, 256), F32), ((STRIP + 128, 128), WIRE)],
        guess, guess.reshape(SEG * SEG * 2, RHS), leaf_map[0, 0], kept=3,
        scratch=[pltpu.VMEM((2, 256, 256), F32), dma((5,))],
    )
    row_k, col_j, col_l = [strip.reshape(128, RHS) for strip in strips]
    partner = swap_near(sent, "tx")
    across_k = swap_far(row_k, "tx")
    across_l = swap_far(col_l, "ty")
    across_j = swap_near(col_j, "ty")
    flat, _ = call(
        stencil_kernel, "stencil", [((SEG * SEG, 2 * RHS), F32), ((SEG, SEG), F32)],
        source.reshape(SEG * SEG * 2, RHS), guess.reshape(SEG * SEG * 2, RHS), coefficient, cost=1.0,
    )
    body = body_map.reshape(512, SEG * SEG)
    own_load, sent_load = call(
        leaf_kernel, "leaf_loads", [((2, 256, RHS), F32), ((2, 192, RHS), WIRE)],
        flat, body, across_j, across_k, across_l, partner, cost=2.5,
        scratch=[pltpu.VMEM((512, 2 * RHS), F32), pltpu.VMEM((128, RHS), F32), pltpu.VMEM((128, RHS), F32)],
    )
    partner, sent_load = lax.optimization_barrier((partner, sent_load))
    partner_load = swap_near(sent_load, "tx")

    face1, keep1, gain1 = call(
        merge_rows_kernel, "merge_rows",
        [((2, 128, 384), F32), ((2, 128, 384), F32), ((2, 256, 128), F32)], own, partner, cost=COSTS[4],
    )
    face1_across = swap_near(face1, "ty")
    load1, keep_load1 = call(
        load_rows_kernel, "load_rows", [((2, 128, RHS), F32)] * 2, own_load, partner_load, gain1, cost=COSTS[0]
    )
    load1_across = swap_near(load1, "ty")
    map2, near2, out_map2, gain2 = call(
        merge_cols_kernel, "merge_cols",
        [((2, 64, 512), F32), ((2, 64, 128), WIRE), ((2, 64, 512), F32), ((2, 128, 256), F32)],
        face1, face1_across, keep1, cost=COSTS[1],
    )
    far_near = from_other_half(near2)
    face2, rest2, out2 = call(
        load_cols_kernel, "load_cols", [((2, 64, 640), F32), ((2, 64, 512), WIRE), ((2, 64, 640), F32)],
        load1, load1_across, keep_load1, gain2, map2, out_map2, cost=COSTS[2],
    )
    face2_mate = swap_near(face2, "ty")
    far_rest = from_other_half(rest2)
    far_near_mate = swap_near(far_near, "ty")
    carried, mine = call(
        top_solve_kernel, "top_solve", [((2, 64, 128), F32), ((2, 64, 512), F32)],
        face2, face2_mate, far_near, far_near_mate, out2, cost=COSTS[3],
    )
    far_rest, carried = lax.optimization_barrier((far_rest, carried))
    far_rest_mate = swap_near(far_rest, "ty")
    top_map, top_out = call(
        top_kernel, "merge_top", [((2, 64, 768), F32), ((2, 64, RHS), F32)],
        carried, mine, far_rest, far_rest_mate,
    )
    return top_map[None, None], top_out[None, None]


def solution(mesh):
    placed = (
        P("tx", "ty", None, None),
        P("tx", "ty", None, None),
        P("tx", "ty"),
        P("tx", "ty", None, None, None),
        P("tx", "ty", None, None, None),
    )
    return jax.shard_map(
        on_device,
        mesh=mesh,
        in_specs=placed,
        out_specs=(P("tx", "ty", None, None, None), P("tx", "ty", None, None, None)),
        check_vma=False,
    )
```
